128 devices in a mesh: tx: 8 (over y, core), ty: 16 (over z, x).
Axes of the slice: x: 4, y: 4, z: 4, core: 2. Of those that a mesh axis runs over, the one named last changes fastest.
Arguments:
- scenes: bfloat16 [256, 128, 384], P(('tx', 'ty')), may hold values from -6 to 6
- foot_tile: int32 [8192], P(('tx', 'ty')), may hold values from 0 to 127, as said below
- foot_offset: int32 [8192], P(('tx', 'ty')), may hold values from 0 to 126, as said below
- foot_count: int32 [8192], P(('tx', 'ty')), may hold values from 1 to 2, as said below
- row_weight: int32 [16384], P(('tx', 'ty')), may hold values from 1 to 8
- stem_weight: bfloat16 [54, 128], replicated, may hold values from -0.875 to 0.875
- stem_bias: float32 [128], replicated, may hold values from -3 to 3
- first_weight: bfloat16 [1152, 256], replicated, may hold values from -0.1875 to 0.1875
- first_scale: float32 [256], replicated, may hold values from 0.5 to 1.5
- first_shift: float32 [256], replicated, may hold values from -2 to 2
- second_weight: bfloat16 [2304, 256], replicated, may hold values from -0.125 to 0.125
- second_scale: float32 [256], replicated, may hold values from 0.5 to 1.5
- second_shift: float32 [256], replicated, may hold values from -2 to 2
Outputs:
- encoded: bfloat16 [1024, 512, 256], P('tx', 'ty')
The draws below stay inside these ranges and needn't reach their ends.
Inputs may be any that keep to these rules, and one draw needn't show every extreme that they name: `foot_tile`: the 64 entries of one device name different tiles; in every draw one tile is named by the first entry of every device. A program may carry tile numbers in any encoding that loses none of them, several to a word included. `foot_offset`: A program may carry offsets in any encoding that loses none of them, several to a word included. `foot_count`: the first entry of every device covers 2 rows. A program may carry counts in any encoding that loses none of them, several to a word included. `row_weight`: A program may carry the weights in any encoding that loses none of them, several to a word included.
All inputs are finite; a program needn't handle non-finite values.
Results may differ from the reference program's by a relative error of at most 0.0053.
Values may be sent and summed in bfloat16 or wider, within the bound.
A program may use at most 128 MiB of HBM per device.

```python
import jax
import jax.numpy as jnp
from jax import lax

BANDS = 6
C1 = 128
C2 = 256
TR = 128
TW = 32
SC_DEV = 2
SR = 64
ENTRIES = 64
ROWS_DEV = 128
CAP = 2
SCENES = 256
ALL_ROWS = 16384
N_TX = 8
N_TY = 16
DEVICES = 128


def draw_foot_tile(key, part):
    key = jax.random.fold_in(key, 21)
    hot_key, popular_key, jitter_key = jax.random.split(key, 3)
    hottest = jax.random.randint(hot_key, (), 0, DEVICES)
    popular = jax.random.randint(popular_key, (DEVICES,), 0, 4)
    jitter = jax.random.randint(jitter_key, (DEVICES, DEVICES), 0, 1024)
    tile_ids = jnp.arange(DEVICES, dtype=jnp.int32)
    scores = (jitter + 300 * popular[None, :]) * DEVICES + tile_ids[None, :]
    scores = jnp.where(tile_ids[None, :] == hottest, 1 << 30, scores)
    ranked, chosen = lax.top_k(scores, ENTRIES)
    return chosen.reshape(DEVICES * ENTRIES).astype(jnp.int32)


def draw_foot_offset(key, part):
    key = jax.random.fold_in(key, 22)
    offsets = jax.random.randint(key, (DEVICES * ENTRIES,), 0, TR - CAP + 1)
    offsets = offsets.at[1].set(TR - CAP)
    offsets = offsets.at[2].set(0)
    return offsets.astype(jnp.int32)


def draw_foot_count(key, part):
    key = jax.random.fold_in(key, 23)
    counts = jax.random.randint(key, (DEVICES, ENTRIES), CAP // 2, CAP + 1)
    counts = counts.at[:, 0].set(CAP)
    counts = counts.at[0, 1].set(CAP // 2)
    return counts.reshape(DEVICES * ENTRIES).astype(jnp.int32)


def place_ends(drawn, own_key, low, high):
    longest = drawn.shape.index(max(drawn.shape))
    spots = []
    for shift in (0, 1):
        where = [jax.random.randint(jax.random.fold_in(own_key, axis), (), 0, length) for axis, length in enumerate(drawn.shape)]
        where[longest] = (where[longest] + shift) % drawn.shape[longest]
        spots.append(tuple(where))
    return drawn.at[spots[0]].set(low).at[spots[1]].set(high)


def steps_of(stream_key, shape, shards, smallest, top_value):
    def one(dim, blocks):
        heights = jax.random.uniform(jax.random.fold_in(jax.random.fold_in(stream_key, 6), dim), (blocks,), jnp.float32, smallest / len(shards), top_value / len(shards))
        return jnp.repeat(jnp.exp(heights), shape[dim] // blocks).reshape((-1,) + (1,) * (len(shape) - dim - 1))

    factor_of = one(*shards[0])
    for cut in shards[1:]:
        factor_of = factor_of * one(*cut)
    return factor_of


def centred(own_key, dims, deviation, bound, cuts=(), held_as=jnp.bfloat16):
    loudness = steps_of(own_key, dims, cuts, -0.22, 0.18) if cuts else 1.0
    entries = jax.random.normal(own_key, dims, jnp.float32) * deviation * loudness
    return jnp.minimum(jnp.maximum(entries, -bound), bound).astype(held_as)


def setup_inputs(seed: int = 0) -> dict:
    key_of = jax.random.split(jax.random.key(seed), 14)
    scenes = centred(key_of[0], (SCENES, 2 * SR, 2 * TW * BANDS), 1.0, 6.0, ((0, 128),))
    foot_tile = draw_foot_tile(jax.random.fold_in(key_of[13], 71), 0)
    foot_offset = draw_foot_offset(jax.random.fold_in(key_of[13], 71), 0)
    foot_count = draw_foot_count(jax.random.fold_in(key_of[13], 71), 0)
    row_weight = place_ends(jax.random.randint(key_of[4], (ALL_ROWS,), 1, 9), jax.random.fold_in(key_of[4], 1), 1, 8).astype(jnp.int32)
    stem_weight = centred(key_of[5], (9 * BANDS, C1), (9 * BANDS) ** -0.5, 0.875)
    stem_bias = centred(key_of[6], (C1,), 0.5, 3.0, (), jnp.float32)
    first_weight = centred(key_of[7], (9 * C1, C2), (9 * C1) ** -0.5, 0.1875)
    first_scale = jnp.clip(1.0 + 0.1 * jax.random.normal(key_of[8], (C2,), jnp.float32), 0.5, 1.5)
    first_shift = centred(key_of[9], (C2,), 0.3, 2.0, (), jnp.float32)
    second_weight = centred(key_of[10], (9 * C2, C2), (9 * C2) ** -0.5, 0.125)
    second_scale = jnp.clip(1.0 + 0.1 * jax.random.normal(key_of[11], (C2,), jnp.float32), 0.5, 1.5)
    second_shift = centred(key_of[12], (C2,), 0.3, 2.0, (), jnp.float32)
    return {"scenes": scenes, "foot_tile": foot_tile, "foot_offset": foot_offset, "foot_count": foot_count, "row_weight": row_weight, "stem_weight": stem_weight, "stem_bias": stem_bias, "first_weight": first_weight, "first_scale": first_scale, "first_shift": first_shift, "second_weight": second_weight, "second_scale": second_scale, "second_shift": second_shift}


def make_strips(scene_block):
    scene_count, height, row_span = scene_block.shape
    padded = jnp.pad(scene_block, ((0, 0), (1, 0), (0, 0)))
    row_pairs = padded[:, :height].reshape(scene_count, height // 2, 2, row_span)
    third_rows = padded[:, 2::2]
    strips = jnp.concatenate([row_pairs, third_rows[:, :, None, :]], axis=2)
    return strips.reshape(scene_count * (height // 2), 3 * row_span)


def stem_rows(strips, stem_weight, stem_bias):
    count_rows = strips.shape[0]
    band_count = stem_weight.shape[0] // 9
    width_in = strips.shape[1] // (3 * band_count)
    width_out = width_in // 2
    pixels = strips.reshape(count_rows, 3, width_in, band_count)
    padded = jnp.pad(pixels, ((0, 0), (0, 0), (1, 0), (0, 0)))
    columns = [padded[:, :, offset:offset + 2 * width_out:2, :] for offset in range(3)]
    tap_stack = jnp.stack(columns, axis=2)
    patches = tap_stack.transpose(0, 3, 1, 2, 4).reshape(count_rows * width_out, 9 * band_count)
    summed = jnp.dot(patches, stem_weight, preferred_element_type=jnp.float32) + stem_bias
    activated = jnp.maximum(summed, 0.0).astype(jnp.bfloat16)
    return activated.reshape(count_rows, width_out * stem_weight.shape[1])


def conv_layer(padded, weight, scale, shift, rows_out, cols_out):
    channels_in = padded.shape[2]
    channels_out = weight.shape[1]
    kernel = weight.reshape(3, 3, channels_in, channels_out).astype(jnp.float32)
    summed = jnp.zeros((rows_out * cols_out, channels_out), jnp.float32)
    for shift_row in range(3):
        for shift_col in range(3):
            window = padded[shift_row:shift_row + rows_out, shift_col:shift_col + cols_out]
            window = window.reshape(rows_out * cols_out, channels_in).astype(jnp.float32)
            summed = summed + jnp.dot(window, kernel[shift_row, shift_col], preferred_element_type=jnp.float32)
    activated = jnp.maximum(summed * scale + shift, 0.0)
    return activated.reshape(rows_out, cols_out, channels_out)


def reference(scenes, foot_tile, foot_offset, foot_count, row_weight, stem_weight, stem_bias,
              first_weight, first_scale, first_shift, second_weight, second_scale, second_shift):
    row_span = scenes.shape[2]
    scene_blocks = scenes.reshape(DEVICES, SC_DEV, 2 * SR, row_span)
    tile_lists = foot_tile.reshape(DEVICES, ENTRIES)
    offset_lists = foot_offset.reshape(DEVICES, ENTRIES)
    count_lists = foot_count.reshape(DEVICES, ENTRIES)
    weight_lists = row_weight.reshape(DEVICES, ROWS_DEV)
    row_index = jnp.arange(ROWS_DEV).astype(jnp.int32)
    slot_index = (row_index % CAP).astype(jnp.int32)
    entry_index = (row_index // CAP).astype(jnp.int32)

    def accumulate(carry, inputs):
        numerator, denominator = carry
        block, tile_list, offset_list, count_list, weight_list = inputs
        features = stem_rows(make_strips(block), stem_weight, stem_bias)
        usable = slot_index < count_list[entry_index]
        landing = (tile_list[entry_index] * TR + offset_list[entry_index] + slot_index).astype(jnp.int32)
        weighting = jnp.where(usable, weight_list, 0).astype(jnp.float32)
        numerator = numerator.at[landing].add(weighting[:, None] * features.astype(jnp.float32))
        denominator = denominator.at[landing].add(weighting)
        return (numerator, denominator), None

    initial = (jnp.zeros((DEVICES * TR, TW * C1), jnp.float32), jnp.zeros((DEVICES * TR,), jnp.float32))
    (numerator, denominator), unused = lax.scan(
        accumulate, initial, (scene_blocks, tile_lists, offset_lists, count_lists, weight_lists))
    blended = (numerator / jnp.maximum(denominator, 1.0)[:, None]).astype(jnp.bfloat16)
    assembled = blended.reshape(N_TX, N_TY, TR, TW, C1).transpose(0, 2, 1, 3, 4).reshape(N_TX * TR, N_TY * TW, C1)
    padded = jnp.pad(assembled, ((2, 2), (2, 2), (0, 0)))

    def one_tile(tile_index):
        grid_row = tile_index // N_TY
        grid_col = tile_index % N_TY
        window = lax.dynamic_slice(padded, (grid_row * TR, grid_col * TW, grid_row * 0), (TR + 4, TW + 4, C1))
        first = conv_layer(window, first_weight, first_scale, first_shift, TR + 2, TW + 2)
        row_global = grid_row * TR - 1 + jnp.arange(TR + 2).astype(jnp.int32)
        col_global = grid_col * TW - 1 + jnp.arange(TW + 2).astype(jnp.int32)
        row_inside = (row_global >= 0) & (row_global < N_TX * TR)
        col_inside = (col_global >= 0) & (col_global < N_TY * TW)
        inside = row_inside[:, None] & col_inside[None, :]
        hidden = jnp.where(inside[:, :, None], first, 0.0).astype(jnp.bfloat16)
        second = conv_layer(hidden, second_weight, second_scale, second_shift, TR, TW)
        return second.astype(jnp.bfloat16)

    tiles_out = lax.map(one_tile, jnp.arange(DEVICES).astype(jnp.int32))
    return tiles_out.reshape(N_TX, N_TY, TR, TW, C2).transpose(0, 2, 1, 3, 4).reshape(N_TX * TR, N_TY * TW, C2)
```

```python
import jax
import jax.numpy as jnp
from jax import lax
from jax.experimental import pallas as pl
from jax.experimental.pallas import tpu as pltpu
from jax.sharding import PartitionSpec as P

TR, TW = 128, 32
NX, NY = 8, 16
DEV = NX * NY
ENT = 64
C1, C2 = 128, 256
PITCH1 = 152
PITCH2 = 40
MB = 32
BF, F32 = jnp.bfloat16, jnp.float32
MESH = pl.DeviceIdType.MESH


def iota(shape, dim):
    return lax.broadcasted_iota(jnp.int32, shape, dim)


def pack_messages(scene, tile, offset, count, rweight, s32, o32, out):
    for c in range(3):
        s32[c, 0:8] = jnp.zeros((8, 128), F32)
        s32[c, 8:264] = scene[:, 128 * c : 128 * c + 128].astype(F32)
    first_row = (iota((ENT, 128), 0) % (ENT // 2)) != 0
    chunks = []
    for p in range(5):
        for c in range(3):
            rows = s32[c, pl.ds(7 + p, ENT, stride=4), :]
            if p == 0:
                rows = jnp.where(first_row, rows, 0.0)
            chunks.append(rows.astype(BF))
    pixels = jnp.concatenate(chunks, axis=1)
    onehot = (iota((DEV, ENT), 0) == tile[...]).astype(F32).astype(BF)
    picked = jnp.dot(onehot, pixels, preferred_element_type=F32)
    for r in range(15):
        o32[pl.ds(r, DEV, stride=16), :] = picked[:, 128 * r : 128 * r + 128]
    both = jnp.broadcast_to(rweight[...].astype(F32), (16, 128)).astype(BF)
    src, dst = iota((128, ENT), 0), iota((128, ENT), 1)
    w0 = jnp.dot(both, (src == 2 * dst).astype(F32).astype(BF), preferred_element_type=F32)[0:1]
    w1 = jnp.dot(both, (src == 2 * dst + 1).astype(F32).astype(BF), preferred_element_type=F32)[0:1]
    row = iota((TR, ENT), 0)
    spread = jnp.where(row == offset[...], w0, 0.0)
    spread += jnp.where(row == offset[...] + 1, jnp.where(count[...] > 1, w1 + 16.0, 0.0), 0.0)
    o32[pl.ds(15, DEV, stride=16), :] = lax.dot_general(
        onehot, spread.astype(BF), (((1,), (1,)), ((), ())), preferred_element_type=F32
    )
    out[...] = o32[...].astype(BF).reshape(DEV, 16, 128)


def build_stem(stem_w, wf, wide):
    wf[...] = jnp.zeros(wf.shape, F32)
    taps = stem_w[...].astype(F32)
    for a in range(3):
        for j in range(8):
            wf[128 * a + 12 * j : 128 * a + 12 * j + 18, 128 * j : 128 * j + 128] = taps[18 * a : 18 * a + 18]
    wide[...] = wf[...].astype(BF)


def blend(arrived, r32, wide, bias, b32, strips):
    r32[...] = arrived[...].astype(F32).reshape(DEV * 16, 128)

    def chunk(r):
        return r32[pl.ds(r, DEV, stride=16), :]

    lane = iota((DEV, 128), 1)
    windows = []
    for p in range(5):
        c0, c1, c2 = chunk(3 * p), chunk(3 * p + 1), chunk(3 * p + 2)
        w0 = jnp.where(lane < 6, 0.0, pltpu.roll(c0, 6, 1))
        w1 = jnp.where(lane < 38, pltpu.roll(c0, 38, 1), pltpu.roll(c1, 38, 1))
        w2 = jnp.where(lane < 70, pltpu.roll(c1, 70, 1), pltpu.roll(c2, 70, 1))
        w3 = pltpu.roll(c2, 102, 1)
        windows.append([w.astype(BF) for w in (w0, w1, w2, w3)])
    code = chunk(15)
    first = jnp.where(code <= 8.0, code, 0.0)
    second = jnp.where(code > 8.0, code - 16.0, 0.0)
    weights = jnp.concatenate([first, second], axis=0).astype(BF)
    contract = (((0,), (0,)), ((), ()))
    total = lax.dot_general(weights, jnp.ones((256, 128), BF), contract, preferred_element_type=F32)
    inverse = 1.0 / jnp.maximum(total, 1.0)
    wide_bias = jnp.concatenate([bias[...]] * 8, axis=1)
    for m in range(4):
        pixels = jnp.concatenate(
            [jnp.concatenate([windows[2 * i + a][m] for a in range(3)], axis=1) for i in range(2)], axis=0
        )
        summed = jnp.dot(pixels, wide[...], preferred_element_type=F32) + wide_bias
        features = jnp.maximum(summed, 0.0).astype(BF)
        numerator = lax.dot_general(weights, features, contract, preferred_element_type=F32)
        for j in range(8):
            column = 8 * m + j
            value = (numerator[:, 128 * j : 128 * j + 128] * inverse).astype(BF)
            start = (column + 2) * PITCH1 + 8
            b32[start : start + TR] = value.astype(F32)
            if column < 2:
                strips[column] = value
            if column >= TW - 2:
                strips[column - TW + 4] = value


def kernel(
    scene_h, tile_h, offset_h, count_h, rweight_h, stem_w_h, bias_h,
    w1_h, scale1_h, shift1_h, w2_h, scale2_h, shift2_h, out_h,
    scene, tile, offset, count, rweight, stem_w, bias, w1, scale1, shift1, w2, scale2, shift2,
    s32, o32, send, recv, r32, wf, wide, b32, strips, edges, got_strips, got_edges, got_corners,
    l1, h32, l2, out,
    in_sem, small_sem, w_sem, a2a_send, a2a_recv, halo_send, halo_recv, ready, out_sem,
):
    tx, ty = lax.axis_index("tx"), lax.axis_index("ty")
    me = tx * NY + ty

    small = [
        (tile_h, tile), (offset_h, offset), (count_h, count), (rweight_h, rweight), (stem_w_h, stem_w), (bias_h, bias),
        (scale1_h, scale1), (shift1_h, shift1), (scale2_h, scale2), (shift2_h, shift2),
    ]
    loads = [pltpu.make_async_copy(scene_h, scene, in_sem)]
    loads += [pltpu.make_async_copy(a, b, small_sem.at[n]) for n, (a, b) in enumerate(small)]
    for copy in loads:
        copy.start()
    weight_loads = []
    for a in range(3):
        for b in range(3):
            source, target = (3 * a + b) * C1, (3 * b + a) * C1
            weight_loads.append(
                pltpu.make_async_copy(w1_h.at[pl.ds(source, C1)], w1.at[pl.ds(target, C1)], w_sem.at[3 * a + b])
            )
    weight_loads.append(pltpu.make_async_copy(w2_h, w2, w_sem.at[9]))
    for copy in weight_loads:
        copy.start()

    barrier = pltpu.get_barrier_semaphore()

    def greet(semaphore, other_tx, other_ty):
        pl.semaphore_signal(semaphore, inc=1, device_id=(other_tx, other_ty), device_id_type=MESH)

    for n in range(1, NX):
        greet(barrier, lax.rem(tx + n, NX), ty)
    for n in range(1, NY):
        greet(barrier, tx, lax.rem(ty + n, NY))

    for copy in loads:
        copy.wait()
    pack_messages(scene, tile, offset, count, rweight, s32, o32, send)

    pl.semaphore_wait(barrier, NX + NY - 2)
    for n in range(1, NX):
        greet(ready, lax.rem(tx + n, NX), ty)
    pl.semaphore_wait(ready, NX - 1)

    def send_one(n, carry):
        other = lax.rem(me + n, DEV)
        pltpu.make_async_remote_copy(
            send.at[other], recv.at[me], a2a_send, a2a_recv,
            device_id=(lax.div(other, NY), lax.rem(other, NY)), device_id_type=MESH,
        ).start()
        return carry

    lax.fori_loop(1, DEV, send_one, 0)
    recv[me] = send[me]
    build_stem(stem_w, wf, wide)
    others = pl.ds(0, DEV - 1)
    pltpu.make_async_remote_copy(
        send.at[others], recv.at[others], a2a_send, a2a_recv, device_id=(tx, ty), device_id_type=MESH
    ).wait()

    blend(recv, r32, wide, bias, b32, strips)

    for side in range(2):
        for r in range(2):
            row = 8 + r + side * (TR - 2)
            edges[side, r] = b32[pl.ds(2 * PITCH1 + row, TW, stride=PITCH1), :].astype(BF)
    up, down = lax.rem(tx + NX - 1, NX), lax.rem(tx + 1, NX)
    left, right = lax.rem(ty + NY - 1, NY), lax.rem(ty + 1, NY)
    half = TW // 2
    near, far = pl.ds(0, half), pl.ds(half, half)
    moves = [
        (edges.at[1], got_edges.at[0], (down, ty)),
        (edges.at[0], got_edges.at[1], (up, ty)),
        (strips.at[pl.ds(2, 2)], got_strips.at[0], (tx, right)),
        (strips.at[pl.ds(0, 2)], got_strips.at[1], (tx, left)),
        (edges.at[1, :, far], got_corners.at[0], (down, right)),
        (edges.at[1, :, near], got_corners.at[1], (down, left)),
        (edges.at[0, :, far], got_corners.at[2], (up, right)),
        (edges.at[0, :, near], got_corners.at[3], (up, left)),
    ]
    halo = [
        pltpu.make_async_remote_copy(
            source, target, halo_send.at[n], halo_recv.at[n], device_id=device, device_id_type=MESH
        )
        for n, (source, target, device) in enumerate(moves)
    ]
    for copy in halo:
        copy.start()
    for copy in halo:
        copy.wait()

    has_up, has_down = tx > 0, tx < NX - 1
    has_left, has_right = ty > 0, ty < NY - 1
    for side, inside in ((0, has_up), (1, has_down)):
        for r in range(2):
            row = 6 + r + side * (TR + 2)
            line = jnp.where(inside, got_edges[side, r].astype(F32), 0.0)
            b32[pl.ds(2 * PITCH1 + row, TW, stride=PITCH1), :] = line
    for side, inside in ((0, has_left), (1, has_right)):
        for c in range(2):
            start = (c + side * (TW + 2)) * PITCH1
            strip = jnp.where(inside, got_strips[side, c].astype(F32), 0.0)
            b32[start + 8 : start + 8 + TR] = strip
    for corner in range(4):
        lower, to_left = corner >= 2, corner % 2 == 0
        inside = (has_down if lower else has_up) & (has_left if to_left else has_right)
        for r in range(2):
            values = jnp.where(inside, got_corners[corner, r].astype(F32), 0.0)
            for c in range(2):
                column = c if to_left else TW + 2 + c
                picked = half - 2 + c if to_left else c
                at = column * PITCH1 + 6 + r + (TR + 2 if lower else 0)
                b32[at : at + 1] = values[picked : picked + 1]

    def lay_column(t, carry):
        start = pl.multiple_of(t * PITCH1, 8)
        for a in range(3):
            l1[t, :, 128 * a : 128 * a + 128] = b32[pl.ds(start + 6 + a, 144), :].astype(BF)
        return carry

    lax.fori_loop(0, TW + 4, lay_column, 0)

    for copy in weight_loads:
        copy.wait()

    rows = iota((144, C2), 0)
    keep_rows = ((rows > 0) | has_up) & ((rows < TR + 1) | has_down)

    def first_conv(t, carry):
        pixels = jnp.concatenate([l1[t], l1[t + 1], l1[t + 2]], axis=1)
        summed = jnp.dot(pixels, w1[...], preferred_element_type=F32)
        value = jnp.maximum(summed * scale1[...] + shift1[...], 0.0).astype(BF).astype(F32)
        inside = ((t > 0) | has_left) & ((t < TW + 1) | has_right)
        value = jnp.where(keep_rows & inside, value, 0.0)
        for c in range(2):
            h32[c, pl.ds(t, TR + 2, stride=PITCH2), :] = value[: TR + 2, 128 * c : 128 * c + 128]
        return carry

    lax.fori_loop(0, TW + 2, first_conv, 0)

    def lay_row(h, carry):
        start = pl.multiple_of(h * PITCH2, 8)
        for b in range(3):
            for c in range(2):
                lanes = 256 * b + 128 * c
                l2[h, :, lanes : lanes + 128] = h32[c, pl.ds(start + b, TW), :].astype(BF)
        return carry

    lax.fori_loop(0, TR + 2, lay_row, 0)

    def second_conv(n, carry):
        y = n * MB
        summed = None
        for a in range(3):
            pixels = l2[pl.ds(y + a, MB)].reshape(MB * TW, 3 * C2)
            part = jnp.dot(pixels, w2[3 * C2 * a : 3 * C2 * (a + 1)], preferred_element_type=F32)
            summed = part if a == 0 else summed + part
        value = jnp.maximum(summed * scale2[...] + shift2[...], 0.0).astype(BF)
        out[pl.ds(y, MB)] = value.reshape(MB, TW, C2)
        pltpu.make_async_copy(out.at[pl.ds(y, MB)], out_h.at[pl.ds(y, MB)], out_sem.at[n]).start()
        return carry

    lax.fori_loop(0, TR // MB, second_conv, 0)
    for n in range(TR // MB):
        pltpu.make_async_copy(out.at[pl.ds(n * MB, MB)], out_h.at[pl.ds(n * MB, MB)], out_sem.at[n]).wait()


def per_device(
    scenes, foot_tile, foot_offset, foot_count, row_weight, stem_weight, stem_bias,
    first_weight, first_scale, first_shift, second_weight, second_scale, second_shift,
):
    args = (
        scenes.reshape(2 * TR, 3 * 128),
        foot_tile.reshape(1, ENT),
        foot_offset.reshape(1, ENT),
        foot_count.reshape(1, ENT),
        row_weight.reshape(1, 128),
        stem_weight,
        stem_bias.reshape(1, C1),
        first_weight,
        first_scale.reshape(1, C2),
        first_shift.reshape(1, C2),
        second_weight,
        second_scale.reshape(1, C2),
        second_shift.reshape(1, C2),
    )
    dma = pltpu.SemaphoreType.DMA
    v = pltpu.VMEM
    scratch = [v(x.shape, x.dtype) for x in args]
    scratch += [
        v((3, 264, 128), F32), v((DEV * 16, 128), F32), v((DEV, 16, 128), BF), v((DEV, 16, 128), BF),
        v((DEV * 16, 128), F32), v((384, 1024), F32), v((384, 1024), BF),
        v(((TW + 4) * PITCH1, 128), F32), v((4, TR, 128), BF), v((2, 2, TW, 128), BF),
        v((2, 2, TR, 128), BF), v((2, 2, TW, 128), BF), v((4, 2, TW // 2, 128), BF),
        v((TW + 4, 144, 384), BF), v((2, (TR + 2) * PITCH2, 128), F32), v((TR + 2, TW, 3 * C2), BF),
        v((TR, TW, C2), BF),
        dma, dma((10,)), dma((10,)), dma, dma, dma((8,)), dma((8,)), pltpu.SemaphoreType.REGULAR, dma((TR // MB,)),
    ]
    return pl.pallas_call(
        kernel,
        out_shape=jax.ShapeDtypeStruct((TR, TW, C2), BF),
        in_specs=[pl.BlockSpec(memory_space=pl.ANY)] * len(args),
        out_specs=pl.BlockSpec(memory_space=pl.ANY),
        scratch_shapes=scratch,
        compiler_params=pltpu.CompilerParams(
            collective_id=0, has_side_effects=True, vmem_limit_bytes=56 * 1024 * 1024
        ),
        cost_estimate=pl.CostEstimate(flops=7_500_000_000, bytes_accessed=6_000_000, transcendentals=0),
    )(*args)


def solution(mesh):
    shared = P()
    split = P(("tx", "ty"))
    in_specs = (P(("tx", "ty"), None, None), split, split, split, split) + (shared,) * 8
    return jax.shard_map(
        per_device, mesh=mesh, in_specs=in_specs, out_specs=P("tx", "ty", None), check_vma=False
    )
```

```python
import jax
import jax.numpy as jnp
from jax import lax
from jax.experimental import pallas as pl
from jax.experimental.pallas import tpu as pltpu
from jax.sharding import PartitionSpec as P

TR, TW = 128, 32
NX, NY = 8, 16
DEV = NX * NY
ENT = 64
C1, C2 = 128, 256
PITCH1 = 152
PITCH2 = 40
CB = 17
MB = 64
BF, F32 = jnp.bfloat16, jnp.float32
MESH = pl.DeviceIdType.MESH


def iota(shape, dim):
    return lax.broadcasted_iota(jnp.int32, shape, dim)


def far_first(tx, ty):
    y, core = tx // 2, lax.rem(tx, 2)
    z, x = ty // 4, lax.rem(ty, 4)
    ys, zs, xs = ([lax.rem(at + d, 4) for d in range(4)] for at in (y, z, x))
    cores = [core, 1 - core]
    steps = [(a, b, c, d) for a in range(4) for b in range(4) for c in range(4) for d in range(2)][1:]
    steps.sort(key=lambda s: (-sum(min(n, 4 - n) for n in s[:3]), s[3], s))
    return [(ys[a] * 2 + cores[d], zs[b] * 4 + xs[c]) for a, b, c, d in steps]


def pack_messages(scene, tile, offset, count, rweight, s32, o32, out):
    for c in range(3):
        s32[c, 0:8] = jnp.zeros((8, 128), F32)
        s32[c, 8:264] = scene[:, 128 * c : 128 * c + 128].astype(F32)
    first_row = (iota((ENT, 128), 0) % (ENT // 2)) != 0
    chunks = []
    for p in range(5):
        for c in range(3):
            rows = s32[c, pl.ds(7 + p, ENT, stride=4), :]
            if p == 0:
                rows = jnp.where(first_row, rows, 0.0)
            chunks.append(rows.astype(BF))
    pixels = jnp.concatenate(chunks, axis=1)
    onehot = (iota((DEV, ENT), 0) == tile[...]).astype(F32).astype(BF)
    picked = jnp.dot(onehot, pixels, preferred_element_type=F32)
    for r in range(15):
        o32[pl.ds(r, DEV, stride=16), :] = picked[:, 128 * r : 128 * r + 128]
    both = jnp.broadcast_to(rweight[...].astype(F32), (16, 128)).astype(BF)
    src, dst = iota((128, ENT), 0), iota((128, ENT), 1)
    w0 = jnp.dot(both, (src == 2 * dst).astype(F32).astype(BF), preferred_element_type=F32)[0:1]
    w1 = jnp.dot(both, (src == 2 * dst + 1).astype(F32).astype(BF), preferred_element_type=F32)[0:1]
    row = iota((TR, ENT), 0)
    spread = jnp.where(row == offset[...], w0, 0.0)
    spread += jnp.where(row == offset[...] + 1, jnp.where(count[...] > 1, w1 + 16.0, 0.0), 0.0)
    o32[pl.ds(15, DEV, stride=16), :] = lax.dot_general(
        onehot, spread.astype(BF), (((1,), (1,)), ((), ())), preferred_element_type=F32
    )
    out[...] = o32[...].astype(BF).reshape(DEV, 16, 128)


def build_stem(stem_w, wf, wide):
    wf[...] = jnp.zeros(wf.shape, F32)
    taps = stem_w[...].astype(F32)
    for a in range(3):
        for j in range(8):
            wf[128 * a + 12 * j : 128 * a + 12 * j + 18, 128 * j : 128 * j + 128] = taps[18 * a : 18 * a + 18]
    wide[...] = wf[...].astype(BF)


def blend(arrived, r32, wide, bias, b32, strips):
    r32[...] = arrived[...].astype(F32).reshape(DEV * 16, 128)

    def chunk(r):
        return r32[pl.ds(r, DEV, stride=16), :]

    lane = iota((DEV, 128), 1)
    windows = []
    for p in range(5):
        c0, c1, c2 = chunk(3 * p), chunk(3 * p + 1), chunk(3 * p + 2)
        w0 = jnp.where(lane < 6, 0.0, pltpu.roll(c0, 6, 1))
        w1 = jnp.where(lane < 38, pltpu.roll(c0, 38, 1), pltpu.roll(c1, 38, 1))
        w2 = jnp.where(lane < 70, pltpu.roll(c1, 70, 1), pltpu.roll(c2, 70, 1))
        w3 = pltpu.roll(c2, 102, 1)
        windows.append([w.astype(BF) for w in (w0, w1, w2, w3)])
    code = chunk(15)
    first = jnp.where(code <= 8.0, code, 0.0)
    second = jnp.where(code > 8.0, code - 16.0, 0.0)
    weights = jnp.concatenate([first, second], axis=0).astype(BF)
    contract = (((0,), (0,)), ((), ()))
    total = lax.dot_general(weights, jnp.ones((256, 128), BF), contract, preferred_element_type=F32)
    inverse = 1.0 / jnp.maximum(total, 1.0)
    wide_bias = jnp.concatenate([bias[...]] * 8, axis=1)
    for m in range(4):
        pixels = jnp.concatenate(
            [jnp.concatenate([windows[2 * i + a][m] for a in range(3)], axis=1) for i in range(2)], axis=0
        )
        summed = jnp.dot(pixels, wide[...], preferred_element_type=F32) + wide_bias
        features = jnp.maximum(summed, 0.0).astype(BF)
        numerator = lax.dot_general(weights, features, contract, preferred_element_type=F32)
        for j in range(8):
            column = 8 * m + j
            value = (numerator[:, 128 * j : 128 * j + 128] * inverse).astype(BF)
            start = (column + 2) * PITCH1 + 8
            b32[start : start + TR] = value.astype(F32)
            if column < 2:
                strips[column] = value
            if column >= TW - 2:
                strips[column - TW + 4] = value


def kernel(
    scene_h, tile_h, offset_h, count_h, rweight_h, stem_w_h, bias_h,
    w1_h, scale1_h, shift1_h, l2,
    scene, tile, offset, count, rweight, stem_w, bias, w1, scale1, shift1,
    s32, o32, send, recv, r32, wf, wide, b32, strips, edges, got_strips, got_edges, got_corners,
    l1, h32,
    in_sem, small_sem, w_sem, a2a_send, a2a_recv, halo_send, halo_recv,
):
    tx, ty = lax.axis_index("tx"), lax.axis_index("ty")
    me = tx * NY + ty

    small = [
        (tile_h, tile), (offset_h, offset), (count_h, count), (rweight_h, rweight), (stem_w_h, stem_w), (bias_h, bias),
        (scale1_h, scale1), (shift1_h, shift1),
    ]
    loads = [pltpu.make_async_copy(scene_h, scene, in_sem)]
    loads += [pltpu.make_async_copy(a, b, small_sem.at[n]) for n, (a, b) in enumerate(small)]
    for copy in loads:
        copy.start()
    weight_loads = []
    for a in range(3):
        for b in range(3):
            source, target = (3 * a + b) * C1, (3 * b + a) * C1
            weight_loads.append(
                pltpu.make_async_copy(w1_h.at[pl.ds(source, C1)], w1.at[pl.ds(target, C1)], w_sem.at[3 * a + b])
            )
    for copy in weight_loads:
        copy.start()

    barrier = pltpu.get_barrier_semaphore()
    places = far_first(tx, ty)
    for place in places:
        pl.semaphore_signal(barrier, inc=1, device_id=place, device_id_type=MESH)

    for copy in loads:
        copy.wait()
    pack_messages(scene, tile, offset, count, rweight, s32, o32, send)

    pl.semaphore_wait(barrier, DEV - 1)
    for place in places:
        pltpu.make_async_remote_copy(
            send.at[place[0] * NY + place[1]], recv.at[me], a2a_send, a2a_recv, device_id=place, device_id_type=MESH
        ).start()
    recv[me] = send[me]
    build_stem(stem_w, wf, wide)
    others = pl.ds(0, DEV - 1)
    exchange = pltpu.make_async_remote_copy(
        send.at[others], recv.at[others], a2a_send, a2a_recv, device_id=(tx, ty), device_id_type=MESH
    )
    exchange.wait_recv()

    blend(recv, r32, wide, bias, b32, strips)

    for side in range(2):
        for r in range(2):
            row = 8 + r + side * (TR - 2)
            edges[side, r] = b32[pl.ds(2 * PITCH1 + row, TW, stride=PITCH1), :].astype(BF)
    has_up, has_down = tx > 0, tx < NX - 1
    has_left, has_right = ty > 0, ty < NY - 1
    half = TW // 2
    near, far = pl.ds(0, half), pl.ds(half, half)
    moves = [
        (strips.at[pl.ds(2, 2)], got_strips.at[0], (0, 1), has_right, has_left),
        (strips.at[pl.ds(0, 2)], got_strips.at[1], (0, -1), has_left, has_right),
        (edges.at[1, :, far], got_corners.at[0], (1, 1), has_down & has_right, has_up & has_left),
        (edges.at[1, :, near], got_corners.at[1], (1, -1), has_down & has_left, has_up & has_right),
        (edges.at[0, :, far], got_corners.at[2], (-1, 1), has_up & has_right, has_down & has_left),
        (edges.at[0, :, near], got_corners.at[3], (-1, -1), has_up & has_left, has_down & has_right),
        (edges.at[1], got_edges.at[0], (1, 0), has_down, has_up),
        (edges.at[0], got_edges.at[1], (-1, 0), has_up, has_down),
    ]
    halo = []
    for n, (source, target, (down, right), sends, receives) in enumerate(moves):
        place = (lax.rem(tx + down + NX, NX), lax.rem(ty + right + NY, NY))
        copy = pltpu.make_async_remote_copy(
            source, target, halo_send.at[n], halo_recv.at[n], device_id=place, device_id_type=MESH
        )
        pl.when(sends)(copy.start)
        halo.append((copy, sends, receives))
    for copy, _, receives in halo:
        pl.when(receives)(copy.wait_recv)

    for side, inside in ((0, has_up), (1, has_down)):
        for r in range(2):
            row = 6 + r + side * (TR + 2)
            line = jnp.where(inside, got_edges[side, r].astype(F32), 0.0)
            b32[pl.ds(2 * PITCH1 + row, TW, stride=PITCH1), :] = line
    for side, inside in ((0, has_left), (1, has_right)):
        for c in range(2):
            start = (c + side * (TW + 2)) * PITCH1
            strip = jnp.where(inside, got_strips[side, c].astype(F32), 0.0)
            b32[start + 8 : start + 8 + TR] = strip
    for corner in range(4):
        lower, to_left = corner >= 2, corner % 2 == 0
        inside = (has_down if lower else has_up) & (has_left if to_left else has_right)
        for r in range(2):
            values = jnp.where(inside, got_corners[corner, r].astype(F32), 0.0)
            for c in range(2):
                column = c if to_left else TW + 2 + c
                picked = half - 2 + c if to_left else c
                at = column * PITCH1 + 6 + r + (TR + 2 if lower else 0)
                b32[at : at + 1] = values[picked : picked + 1]

    def lay_column(t, carry):
        start = pl.multiple_of(t * PITCH1, 8)
        for a in range(3):
            l1[t, :, 128 * a : 128 * a + 128] = b32[pl.ds(start + 6 + a, 144), :].astype(BF)
        return carry

    lax.fori_loop(0, TW + 4, lay_column, 0)

    for copy in weight_loads:
        copy.wait()

    rows = iota((144, C2), 0)
    keep_rows = ((rows > 0) | has_up) & ((rows < TR + 1) | has_down)

    def first_conv(step, carry):
        t = step * CB
        pixels = jnp.concatenate([l1[pl.ds(t + b, CB)].reshape(CB * 144, 3 * C1) for b in range(3)], axis=1)
        summed = jnp.dot(pixels, w1[...], preferred_element_type=F32)
        value = jnp.maximum(summed * scale1[...] + shift1[...], 0.0).astype(BF).astype(F32)
        for n in range(CB):
            inside = ((t + n > 0) | has_left) & ((t + n < TW + 1) | has_right)
            kept = jnp.where(keep_rows & inside, value[144 * n : 144 * n + 144], 0.0)
            for c in range(2):
                h32[c, pl.ds(t + n, TR + 2, stride=PITCH2), :] = kept[: TR + 2, 128 * c : 128 * c + 128]
        return carry

    lax.fori_loop(0, (TW + 2) // CB, first_conv, 0)

    def lay_row(h, carry):
        start = pl.multiple_of(h * PITCH2, 8)
        for b in range(3):
            for c in range(2):
                lanes = 256 * b + 128 * c
                l2[h, :, lanes : lanes + 128] = h32[c, pl.ds(start + b, TW), :].astype(BF)
        return carry

    lax.fori_loop(0, TR + 2, lay_row, 0)

    exchange.wait_send()
    for copy, sends, _ in halo:
        pl.when(sends)(copy.wait_send)


def second_kernel(l2, w2, scale2, shift2, out_h, out, out_sem):
    def move(n):
        part = pl.ds(n * MB, MB)
        return pltpu.make_async_copy(out.at[part], out_h.at[part], out_sem.at[n])

    for n in range(TR // MB):
        y = n * MB
        summed = None
        for a in range(3):
            pixels = l2[pl.ds(y + a, MB)].reshape(MB * TW, 3 * C2)
            part = jnp.dot(pixels, w2[3 * C2 * a : 3 * C2 * (a + 1)], preferred_element_type=F32)
            summed = part if a == 0 else summed + part
        value = jnp.maximum(summed * scale2[...] + shift2[...], 0.0).astype(BF)
        out[pl.ds(y, MB)] = value.reshape(MB, TW, C2)
        move(n).start()
    for n in range(TR // MB):
        move(n).wait()


def per_device(
    scenes, foot_tile, foot_offset, foot_count, row_weight, stem_weight, stem_bias,
    first_weight, first_scale, first_shift, second_weight, second_scale, second_shift,
):
    args = (
        scenes.reshape(2 * TR, 3 * 128),
        foot_tile.reshape(1, ENT),
        foot_offset.reshape(1, ENT),
        foot_count.reshape(1, ENT),
        row_weight.reshape(1, 128),
        stem_weight,
        stem_bias.reshape(1, C1),
        first_weight,
        first_scale.reshape(1, C2),
        first_shift.reshape(1, C2),
    )
    dma = pltpu.SemaphoreType.DMA
    v = pltpu.VMEM
    scratch = [v(x.shape, x.dtype) for x in args]
    scratch += [
        v((3, 264, 128), F32), v((DEV * 16, 128), F32), v((DEV, 16, 128), BF), v((DEV, 16, 128), BF),
        v((DEV * 16, 128), F32), v((384, 1024), F32), v((384, 1024), BF),
        v(((TW + 4) * PITCH1, 128), F32), v((4, TR, 128), BF), v((2, 2, TW, 128), BF),
        v((2, 2, TR, 128), BF), v((2, 2, TW, 128), BF), v((4, 2, TW // 2, 128), BF),
        v((TW + 4, 144, 384), BF), v((2, (TR + 2) * PITCH2, 128), F32),
        dma, dma((8,)), dma((9,)), dma, dma, dma((8,)), dma((8,)),
    ]
    hidden = pl.pallas_call(
        kernel,
        out_shape=jax.ShapeDtypeStruct((TR + 2, TW, 3 * C2), BF),
        in_specs=[pl.BlockSpec(memory_space=pltpu.HBM)] * len(args),
        out_specs=pl.BlockSpec(memory_space=v),
        scratch_shapes=scratch,
        compiler_params=pltpu.CompilerParams(
            collective_id=0, has_side_effects=True, vmem_limit_bytes=44 * 1024 * 1024
        ),
        cost_estimate=pl.CostEstimate(flops=2_700_000_000, bytes_accessed=2_000_000, transcendentals=0),
    )(*[pltpu.with_memory_space_constraint(x, pltpu.HBM) for x in args])
    return pl.pallas_call(
        second_kernel,
        out_shape=jax.ShapeDtypeStruct((TR, TW, C2), BF),
        in_specs=[pl.BlockSpec(memory_space=v)] * 4,
        out_specs=pl.BlockSpec(memory_space=pl.ANY),
        scratch_shapes=[v((TR, TW, C2), BF), dma((TR // MB,))],
        compiler_params=pltpu.CompilerParams(vmem_limit_bytes=32 * 1024 * 1024),
        cost_estimate=pl.CostEstimate(flops=4_800_000_000, bytes_accessed=3_000_000, transcendentals=0),
    )(hidden, second_weight, second_scale.reshape(1, C2), second_shift.reshape(1, C2))


def solution(mesh):
    shared = P()
    split = P(("tx", "ty"))
    in_specs = (P(("tx", "ty"), None, None), split, split, split, split) + (shared,) * 8
    return jax.shard_map(
        per_device, mesh=mesh, in_specs=in_specs, out_specs=P("tx", "ty", None), check_vma=False
    )
```

```python
import jax
import jax.numpy as jnp
from jax import lax
from jax.experimental import pallas as pl
from jax.experimental.pallas import tpu as pltpu
from jax.sharding import PartitionSpec as P

TR, TW = 128, 32
NX, NY = 8, 16
DEV = NX * NY
ENT = 64
C1, C2 = 128, 256
PITCH1 = 152
PITCH2 = 40
MID = 112
CB = 15
MB = 32
BF, F32 = jnp.bfloat16, jnp.float32
MESH = pl.DeviceIdType.MESH


def iota(shape, dim):
    return lax.broadcasted_iota(jnp.int32, shape, dim)


def far_first(tx, ty):
    y, core = tx // 2, lax.rem(tx, 2)
    z, x = ty // 4, lax.rem(ty, 4)
    ys, zs, xs = ([lax.rem(at + d, 4) for d in range(4)] for at in (y, z, x))
    cores = [core, 1 - core]
    steps = [(a, b, c, d) for a in range(4) for b in range(4) for c in range(4) for d in range(2)][1:]
    steps.sort(key=lambda s: (-sum(min(n, 4 - n) for n in s[:3]), s[3], s))
    return [(ys[a] * 2 + cores[d], zs[b] * 4 + xs[c]) for a, b, c, d in steps]


def pack_messages(scene, tile, offset, count, rweight, s32, o32, out):
    for c in range(3):
        s32[c, 0:8] = jnp.zeros((8, 128), F32)
        s32[c, 8:264] = scene[:, 128 * c : 128 * c + 128].astype(F32)
    first_row = (iota((ENT, 128), 0) % (ENT // 2)) != 0
    chunks = []
    for p in range(5):
        for c in range(3):
            rows = s32[c, pl.ds(7 + p, ENT, stride=4), :]
            if p == 0:
                rows = jnp.where(first_row, rows, 0.0)
            chunks.append(rows.astype(BF))
    pixels = jnp.concatenate(chunks, axis=1)
    onehot = (iota((DEV, ENT), 0) == tile[...]).astype(F32).astype(BF)
    picked = jnp.dot(onehot, pixels, preferred_element_type=F32)
    for r in range(15):
        o32[pl.ds(r, DEV, stride=16), :] = picked[:, 128 * r : 128 * r + 128]
    both = jnp.broadcast_to(rweight[...].astype(F32), (16, 128)).astype(BF)
    src, dst = iota((128, ENT), 0), iota((128, ENT), 1)
    w0 = jnp.dot(both, (src == 2 * dst).astype(F32).astype(BF), preferred_element_type=F32)[0:1]
    w1 = jnp.dot(both, (src == 2 * dst + 1).astype(F32).astype(BF), preferred_element_type=F32)[0:1]
    row = iota((TR, ENT), 0)
    spread = jnp.where(row == offset[...], w0, 0.0)
    spread += jnp.where(row == offset[...] + 1, jnp.where(count[...] > 1, w1 + 16.0, 0.0), 0.0)
    o32[pl.ds(15, DEV, stride=16), :] = lax.dot_general(
        onehot, spread.astype(BF), (((1,), (1,)), ((), ())), preferred_element_type=F32
    )
    out[...] = o32[...].astype(BF).reshape(DEV, 16, 128)


def build_stem(stem_w, wf, wide):
    wf[...] = jnp.zeros(wf.shape, F32)
    taps = stem_w[...].astype(F32)
    for a in range(3):
        for j in range(8):
            wf[128 * a + 12 * j : 128 * a + 12 * j + 18, 128 * j : 128 * j + 128] = taps[18 * a : 18 * a + 18]
    wide[...] = wf[...].astype(BF)


def blend(arrived, r32, wide, bias, b32, strips):
    r32[...] = arrived[...].astype(F32).reshape(DEV * 16, 128)

    def chunk(r):
        return r32[pl.ds(r, DEV, stride=16), :]

    lane = iota((DEV, 128), 1)
    windows = []
    for p in range(5):
        c0, c1, c2 = chunk(3 * p), chunk(3 * p + 1), chunk(3 * p + 2)
        w0 = jnp.where(lane < 6, 0.0, pltpu.roll(c0, 6, 1))
        w1 = jnp.where(lane < 38, pltpu.roll(c0, 38, 1), pltpu.roll(c1, 38, 1))
        w2 = jnp.where(lane < 70, pltpu.roll(c1, 70, 1), pltpu.roll(c2, 70, 1))
        w3 = pltpu.roll(c2, 102, 1)
        windows.append([w.astype(BF) for w in (w0, w1, w2, w3)])
    code = chunk(15)
    first = jnp.where(code <= 8.0, code, 0.0)
    second = jnp.where(code > 8.0, code - 16.0, 0.0)
    weights = jnp.concatenate([first, second], axis=0).astype(BF)
    contract = (((0,), (0,)), ((), ()))
    total = lax.dot_general(weights, jnp.ones((256, 128), BF), contract, preferred_element_type=F32)
    inverse = 1.0 / jnp.maximum(total, 1.0)
    wide_bias = jnp.concatenate([bias[...]] * 8, axis=1)
    for m in range(4):
        pixels = jnp.concatenate(
            [jnp.concatenate([windows[2 * i + a][m] for a in range(3)], axis=1) for i in range(2)], axis=0
        )
        summed = jnp.dot(pixels, wide[...], preferred_element_type=F32) + wide_bias
        features = jnp.maximum(summed, 0.0).astype(BF)
        numerator = lax.dot_general(weights, features, contract, preferred_element_type=F32)
        for j in range(8):
            column = 8 * m + j
            value = (numerator[:, 128 * j : 128 * j + 128] * inverse).astype(BF)
            start = (column + 2) * PITCH1 + 8
            b32[start : start + TR] = value.astype(F32)
            if column < 2:
                strips[column] = value
            if column >= TW - 2:
                strips[column - TW + 4] = value


def kernel(
    scene_h, tile_h, offset_h, count_h, rweight_h, stem_w_h, bias_h,
    w1_h, scale1_h, shift1_h, l2,
    scene, tile, offset, count, rweight, stem_w, bias, w1, scale1, shift1,
    s32, o32, send, recv, r32, wf, wide, b32, strips, edges, got_strips, got_edges, got_corners,
    middle, ends, h32,
    in_sem, small_sem, w_sem, a2a_send, a2a_recv, halo_send, halo_recv,
):
    tx, ty = lax.axis_index("tx"), lax.axis_index("ty")
    me = tx * NY + ty

    small = [
        (tile_h, tile), (offset_h, offset), (count_h, count), (rweight_h, rweight), (stem_w_h, stem_w), (bias_h, bias),
        (scale1_h, scale1), (shift1_h, shift1),
    ]
    loads = [pltpu.make_async_copy(scene_h, scene, in_sem)]
    loads += [pltpu.make_async_copy(a, b, small_sem.at[n]) for n, (a, b) in enumerate(small)]
    for copy in loads:
        copy.start()
    weight_loads = []
    for a in range(3):
        for b in range(3):
            source, target = (3 * a + b) * C1, (3 * b + a) * C1
            weight_loads.append(
                pltpu.make_async_copy(w1_h.at[pl.ds(source, C1)], w1.at[pl.ds(target, C1)], w_sem.at[3 * a + b])
            )
    for copy in weight_loads:
        copy.start()

    barrier = pltpu.get_barrier_semaphore()
    places = far_first(tx, ty)
    for place in places:
        pl.semaphore_signal(barrier, inc=1, device_id=place, device_id_type=MESH)

    for copy in loads:
        copy.wait()
    pack_messages(scene, tile, offset, count, rweight, s32, o32, send)

    pl.semaphore_wait(barrier, DEV - 1)
    for place in places:
        pltpu.make_async_remote_copy(
            send.at[place[0] * NY + place[1]], recv.at[me], a2a_send, a2a_recv, device_id=place, device_id_type=MESH
        ).start()
    recv[me] = send[me]
    build_stem(stem_w, wf, wide)
    others = pl.ds(0, DEV - 1)
    exchange = pltpu.make_async_remote_copy(
        send.at[others], recv.at[others], a2a_send, a2a_recv, device_id=(tx, ty), device_id_type=MESH
    )
    exchange.wait_recv()

    blend(recv, r32, wide, bias, b32, strips)

    for side in range(2):
        for r in range(2):
            row = 8 + r + side * (TR - 2)
            edges[side, r] = b32[pl.ds(2 * PITCH1 + row, TW, stride=PITCH1), :].astype(BF)
    has_up, has_down = tx > 0, tx < NX - 1
    has_left, has_right = ty > 0, ty < NY - 1
    half = TW // 2
    near, far = pl.ds(0, half), pl.ds(half, half)
    moves = [
        (strips.at[pl.ds(2, 2)], got_strips.at[0], (0, 1), has_right, has_left),
        (strips.at[pl.ds(0, 2)], got_strips.at[1], (0, -1), has_left, has_right),
        (edges.at[1, :, far], got_corners.at[0], (1, 1), has_down & has_right, has_up & has_left),
        (edges.at[1, :, near], got_corners.at[1], (1, -1), has_down & has_left, has_up & has_right),
        (edges.at[0, :, far], got_corners.at[2], (-1, 1), has_up & has_right, has_down & has_left),
        (edges.at[0, :, near], got_corners.at[3], (-1, -1), has_up & has_left, has_down & has_right),
        (edges.at[1], got_edges.at[0], (1, 0), has_down, has_up),
        (edges.at[0], got_edges.at[1], (-1, 0), has_up, has_down),
    ]
    halo = []
    for n, (source, target, (down, right), sends, receives) in enumerate(moves):
        place = (lax.rem(tx + down + NX, NX), lax.rem(ty + right + NY, NY))
        copy = pltpu.make_async_remote_copy(
            source, target, halo_send.at[n], halo_recv.at[n], device_id=place, device_id_type=MESH
        )
        pl.when(sends)(copy.start)
        halo.append((copy, sends, receives))
    def lay_middle(t):
        for a in range(3):
            start = pl.multiple_of(t * PITCH1, 8) + 22 + a
            middle[t, :, 128 * a : 128 * a + 128] = b32[pl.ds(start, MID), :].astype(BF)

    def lay_ends(t):
        for a in range(3):
            for n in range(2):
                start = pl.multiple_of(t * PITCH1, 8) + 6 + a + 128 * n
                ends[t, 16 * n : 16 * n + 16, 128 * a : 128 * a + 128] = b32[pl.ds(start, 16), :].astype(BF)

    def first_conv(source, t, columns):
        height = source.shape[1]
        pixels = [source[pl.ds(t + b, columns)].reshape(columns * height, 3 * C1) for b in range(3)]
        summed = jnp.dot(jnp.concatenate(pixels, axis=1), w1[...], preferred_element_type=F32)
        value = jnp.maximum(summed * scale1[...] + shift1[...], 0.0).astype(BF).astype(F32)
        return value.reshape(columns, height, C2)

    def loop(start, stop, step, unroll):
        def body(n, carry):
            step(n)
            return carry

        lax.fori_loop(start, stop, body, 0, unroll=unroll)

    loop(2, TW + 2, lay_middle, 5)
    for copy in weight_loads:
        copy.wait()

    def middle_block(n):
        t = 2 + n * CB
        value = first_conv(middle, t, CB)
        for m in range(CB):
            for c in range(2):
                h32[c, pl.ds(16 * PITCH2 + t + m, MID, stride=PITCH2), :] = value[m, :, 128 * c : 128 * c + 128]

    loop(0, (TW - 2) // CB, middle_block, 1)

    for copy, _, receives in halo:
        pl.when(receives)(copy.wait_recv)

    for side, inside in ((0, has_up), (1, has_down)):
        for r in range(2):
            row = 6 + r + side * (TR + 2)
            line = jnp.where(inside, got_edges[side, r].astype(F32), 0.0)
            b32[pl.ds(2 * PITCH1 + row, TW, stride=PITCH1), :] = line
    for side, inside in ((0, has_left), (1, has_right)):
        for c in range(2):
            start = (c + side * (TW + 2)) * PITCH1
            strip = jnp.where(inside, got_strips[side, c].astype(F32), 0.0)
            b32[start + 8 : start + 8 + TR] = strip
    for corner in range(4):
        lower, to_left = corner >= 2, corner % 2 == 0
        inside = (has_down if lower else has_up) & (has_left if to_left else has_right)
        for r in range(2):
            values = jnp.where(inside, got_corners[corner, r].astype(F32), 0.0)
            for c in range(2):
                column = c if to_left else TW + 2 + c
                picked = half - 2 + c if to_left else c
                at = column * PITCH1 + 6 + r + (TR + 2 if lower else 0)
                b32[at : at + 1] = values[picked : picked + 1]

    loop(0, TW + 4, lay_ends, 4)
    for t in (0, 1, TW + 2, TW + 3):
        lay_middle(t)

    for t, inside in ((0, has_left), (TW, has_right)):
        value = first_conv(middle, t, 2)
        for m in range(2):
            kept = value[m]
            if t + m in (0, TW + 1):
                kept = jnp.where(inside, kept, 0.0)
            for c in range(2):
                h32[c, pl.ds(16 * PITCH2 + t + m, MID, stride=PITCH2), :] = kept[:, 128 * c : 128 * c + 128]

    rows = iota((32, C2), 0)
    keep_rows = ((rows > 0) | has_up) & ((rows < 17) | has_down)
    value = first_conv(ends, 0, TW + 2)
    for t in range(TW + 2):
        keep = keep_rows
        if t in (0, TW + 1):
            keep = keep & (has_right if t else has_left)
        kept = jnp.where(keep, value[t], 0.0)
        for c in range(2):
            lanes = slice(128 * c, 128 * c + 128)
            h32[c, pl.ds(t, 16, stride=PITCH2), :] = kept[:16, lanes]
            h32[c, pl.ds(128 * PITCH2 + t, 2, stride=PITCH2), :] = kept[16:18, lanes]

    def lay_row(h):
        start = pl.multiple_of(h * PITCH2, 8)
        for b in range(3):
            for c in range(2):
                lanes = 256 * b + 128 * c
                l2[h, :, lanes : lanes + 128] = h32[c, pl.ds(start + b, TW), :].astype(BF)

    loop(0, TR + 2, lay_row, 5)

    exchange.wait_send()
    for copy, sends, _ in halo:
        pl.when(sends)(copy.wait_send)


def second_kernel(l2, w2, scale2, shift2, out_h, out, out_sem):
    def move(n):
        part = pl.ds(n * MB, MB)
        return pltpu.make_async_copy(out.at[part], out_h.at[part], out_sem.at[n])

    for n in range(TR // MB):
        y = n * MB
        summed = None
        for a in range(3):
            pixels = l2[pl.ds(y + a, MB)].reshape(MB * TW, 3 * C2)
            part = jnp.dot(pixels, w2[3 * C2 * a : 3 * C2 * (a + 1)], preferred_element_type=F32)
            summed = part if a == 0 else summed + part
        value = jnp.maximum(summed * scale2[...] + shift2[...], 0.0).astype(BF)
        out[pl.ds(y, MB)] = value.reshape(MB, TW, C2)
        move(n).start()
    for n in range(TR // MB):
        move(n).wait()


def per_device(
    scenes, foot_tile, foot_offset, foot_count, row_weight, stem_weight, stem_bias,
    first_weight, first_scale, first_shift, second_weight, second_scale, second_shift,
):
    args = (
        scenes.reshape(2 * TR, 3 * 128),
        foot_tile.reshape(1, ENT),
        foot_offset.reshape(1, ENT),
        foot_count.reshape(1, ENT),
        row_weight.reshape(1, 128),
        stem_weight,
        stem_bias.reshape(1, C1),
        first_weight,
        first_scale.reshape(1, C2),
        first_shift.reshape(1, C2),
    )
    dma = pltpu.SemaphoreType.DMA
    v = pltpu.VMEM
    scratch = [v(x.shape, x.dtype) for x in args]
    scratch += [
        v((3, 264, 128), F32), v((DEV * 16, 128), F32), v((DEV, 16, 128), BF), v((DEV, 16, 128), BF),
        v((DEV * 16, 128), F32), v((384, 1024), F32), v((384, 1024), BF),
        v(((TW + 4) * PITCH1, 128), F32), v((4, TR, 128), BF), v((2, 2, TW, 128), BF),
        v((2, 2, TR, 128), BF), v((2, 2, TW, 128), BF), v((4, 2, TW // 2, 128), BF),
        v((TW + 4, MID, 384), BF), v((TW + 4, 32, 384), BF), v((2, (TR + 2) * PITCH2, 128), F32),
        dma, dma((8,)), dma((9,)), dma, dma, dma((8,)), dma((8,)),
    ]
    hidden = pl.pallas_call(
        kernel,
        out_shape=jax.ShapeDtypeStruct((TR + 2, TW, 3 * C2), BF),
        in_specs=[pl.BlockSpec(memory_space=pltpu.HBM)] * len(args),
        out_specs=pl.BlockSpec(memory_space=v),
        scratch_shapes=scratch,
        compiler_params=pltpu.CompilerParams(
            collective_id=0, has_side_effects=True, vmem_limit_bytes=44 * 1024 * 1024
        ),
        cost_estimate=pl.CostEstimate(flops=2_700_000_000, bytes_accessed=2_000_000, transcendentals=0),
    )(*[pltpu.with_memory_space_constraint(x, pltpu.HBM) for x in args])
    return pl.pallas_call(
        second_kernel,
        out_shape=jax.ShapeDtypeStruct((TR, TW, C2), BF),
        in_specs=[pl.BlockSpec(memory_space=v)] * 4,
        out_specs=pl.BlockSpec(memory_space=pl.ANY),
        scratch_shapes=[v((TR, TW, C2), BF), dma((TR // MB,))],
        compiler_params=pltpu.CompilerParams(vmem_limit_bytes=32 * 1024 * 1024),
        cost_estimate=pl.CostEstimate(flops=4_800_000_000, bytes_accessed=3_000_000, transcendentals=0),
    )(hidden, second_weight, second_scale.reshape(1, C2), second_shift.reshape(1, C2))


def solution(mesh):
    shared = P()
    split = P(("tx", "ty"))
    in_specs = (P(("tx", "ty"), None, None), split, split, split, split) + (shared,) * 8
    return jax.shard_map(
        per_device, mesh=mesh, in_specs=in_specs, out_specs=P("tx", "ty", None), check_vma=False
    )
```

```python
import jax
import jax.numpy as jnp
from jax import lax
from jax.experimental import pallas as pl
from jax.experimental.pallas import tpu as pltpu
from jax.sharding import PartitionSpec as P

TR, TW = 128, 32
NX, NY = 8, 16
DEV = NX * NY
ENT = 64
C1, C2 = 128, 256
PITCH1 = 152
PITCH2 = 40
MID = 112
CB = 15
PARTS = (32, 32, 32, 32)
BF, F32 = jnp.bfloat16, jnp.float32
MESH = pl.DeviceIdType.MESH


def iota(shape, dim):
    return lax.broadcasted_iota(jnp.int32, shape, dim)


def far_first(tx, ty):
    y, core = tx // 2, lax.rem(tx, 2)
    z, x = ty // 4, lax.rem(ty, 4)
    ys, zs, xs = ([lax.rem(at + d, 4) for d in range(4)] for at in (y, z, x))
    cores = [core, 1 - core]
    steps = [(a, b, c, d) for a in range(4) for b in range(4) for c in range(4) for d in range(2)][1:]
    steps.sort(key=lambda s: (-sum(min(n, 4 - n) for n in s[:3]), s[3], s))
    return [(ys[a] * 2 + cores[d], zs[b] * 4 + xs[c]) for a, b, c, d in steps]


def pack_messages(scene, tile, offset, count, rweight, s32, o32, out):
    for c in range(3):
        s32[c, 0:8] = jnp.zeros((8, 128), F32)
        s32[c, 8:264] = scene[:, 128 * c : 128 * c + 128].astype(F32)
    first_row = (iota((ENT, 128), 0) % (ENT // 2)) != 0
    chunks = []
    for p in range(5):
        for c in range(3):
            rows = s32[c, pl.ds(7 + p, ENT, stride=4), :]
            if p == 0:
                rows = jnp.where(first_row, rows, 0.0)
            chunks.append(rows.astype(BF))
    pixels = jnp.concatenate(chunks, axis=1)
    onehot = (iota((DEV, ENT), 0) == tile[...]).astype(F32).astype(BF)
    picked = jnp.dot(onehot, pixels, preferred_element_type=F32)
    for r in range(15):
        o32[pl.ds(r, DEV, stride=16), :] = picked[:, 128 * r : 128 * r + 128]
    both = jnp.broadcast_to(rweight[...].astype(F32), (16, 128)).astype(BF)
    src, dst = iota((128, ENT), 0), iota((128, ENT), 1)
    w0 = jnp.dot(both, (src == 2 * dst).astype(F32).astype(BF), preferred_element_type=F32)[0:1]
    w1 = jnp.dot(both, (src == 2 * dst + 1).astype(F32).astype(BF), preferred_element_type=F32)[0:1]
    row = iota((TR, ENT), 0)
    spread = jnp.where(row == offset[...], w0, 0.0)
    spread += jnp.where(row == offset[...] + 1, jnp.where(count[...] > 1, w1 + 16.0, 0.0), 0.0)
    o32[pl.ds(15, DEV, stride=16), :] = lax.dot_general(
        onehot, spread.astype(BF), (((1,), (1,)), ((), ())), preferred_element_type=F32
    )
    out[...] = o32[...].astype(BF).reshape(DEV, 16, 128)


def build_stem(stem_w, wf, wide):
    wf[...] = jnp.zeros(wf.shape, F32)
    taps = stem_w[...].astype(F32)
    for a in range(3):
        for j in range(8):
            wf[128 * a + 12 * j : 128 * a + 12 * j + 18, 128 * j : 128 * j + 128] = taps[18 * a : 18 * a + 18]
    wide[...] = wf[...].astype(BF)


def blend(arrived, r32, wide, bias, b32, strips):
    r32[...] = arrived[...].astype(F32).reshape(DEV * 16, 128)

    def chunk(r):
        return r32[pl.ds(r, DEV, stride=16), :]

    lane = iota((DEV, 128), 1)
    windows = []
    for p in range(5):
        c0, c1, c2 = chunk(3 * p), chunk(3 * p + 1), chunk(3 * p + 2)
        w0 = jnp.where(lane < 6, 0.0, pltpu.roll(c0, 6, 1))
        w1 = jnp.where(lane < 38, pltpu.roll(c0, 38, 1), pltpu.roll(c1, 38, 1))
        w2 = jnp.where(lane < 70, pltpu.roll(c1, 70, 1), pltpu.roll(c2, 70, 1))
        w3 = pltpu.roll(c2, 102, 1)
        windows.append([w.astype(BF) for w in (w0, w1, w2, w3)])
    code = chunk(15)
    first = jnp.where(code <= 8.0, code, 0.0)
    second = jnp.where(code > 8.0, code - 16.0, 0.0)
    weights = jnp.concatenate([first, second], axis=0).astype(BF)
    contract = (((0,), (0,)), ((), ()))
    total = lax.dot_general(weights, jnp.ones((256, 128), BF), contract, preferred_element_type=F32)
    inverse = 1.0 / jnp.maximum(total, 1.0)
    wide_bias = jnp.concatenate([bias[...]] * 8, axis=1)
    for m in range(4):
        pixels = jnp.concatenate(
            [jnp.concatenate([windows[2 * i + a][m] for a in range(3)], axis=1) for i in range(2)], axis=0
        )
        summed = jnp.dot(pixels, wide[...], preferred_element_type=F32) + wide_bias
        features = jnp.maximum(summed, 0.0).astype(BF)
        numerator = lax.dot_general(weights, features, contract, preferred_element_type=F32)
        for j in range(8):
            column = 8 * m + j
            value = (numerator[:, 128 * j : 128 * j + 128] * inverse).astype(BF)
            start = (column + 2) * PITCH1 + 8
            b32[start : start + TR] = value.astype(F32)
            if column < 2:
                strips[column] = value
            if column >= TW - 2:
                strips[column - TW + 4] = value


def kernel(
    scene_h, tile_h, offset_h, count_h, rweight_h, stem_w_h, bias_h,
    w1_h, scale1_h, shift1_h, h32,
    scene, tile, offset, count, rweight, stem_w, bias, w1, scale1, shift1,
    s32, o32, send, recv, r32, wf, wide, b32, strips, edges, got_strips, got_edges, got_corners,
    middle, ends,
    in_sem, small_sem, w_sem, a2a_send, a2a_recv, halo_send, halo_recv,
):
    tx, ty = lax.axis_index("tx"), lax.axis_index("ty")
    me = tx * NY + ty

    small = [
        (tile_h, tile), (offset_h, offset), (count_h, count), (rweight_h, rweight), (stem_w_h, stem_w), (bias_h, bias),
        (scale1_h, scale1), (shift1_h, shift1),
    ]
    loads = [pltpu.make_async_copy(scene_h, scene, in_sem)]
    loads += [pltpu.make_async_copy(a, b, small_sem.at[n]) for n, (a, b) in enumerate(small)]
    for copy in loads:
        copy.start()
    weight_loads = []
    for a in range(3):
        for b in range(3):
            source, target = (3 * a + b) * C1, (3 * b + a) * C1
            weight_loads.append(
                pltpu.make_async_copy(w1_h.at[pl.ds(source, C1)], w1.at[pl.ds(target, C1)], w_sem.at[3 * a + b])
            )
    for copy in weight_loads:
        copy.start()

    barrier = pltpu.get_barrier_semaphore()
    places = far_first(tx, ty)
    for place in places:
        pl.semaphore_signal(barrier, inc=1, device_id=place, device_id_type=MESH)

    for copy in loads:
        copy.wait()
    pack_messages(scene, tile, offset, count, rweight, s32, o32, send)

    pl.semaphore_wait(barrier, DEV - 1)
    for place in places:
        pltpu.make_async_remote_copy(
            send.at[place[0] * NY + place[1]], recv.at[me], a2a_send, a2a_recv, device_id=place, device_id_type=MESH
        ).start()
    recv[me] = send[me]
    build_stem(stem_w, wf, wide)
    others = pl.ds(0, DEV - 1)
    exchange = pltpu.make_async_remote_copy(
        send.at[others], recv.at[others], a2a_send, a2a_recv, device_id=(tx, ty), device_id_type=MESH
    )
    exchange.wait_recv()

    blend(recv, r32, wide, bias, b32, strips)

    for side in range(2):
        for r in range(2):
            row = 8 + r + side * (TR - 2)
            edges[side, r] = b32[pl.ds(2 * PITCH1 + row, TW, stride=PITCH1), :].astype(BF)
    has_up, has_down = tx > 0, tx < NX - 1
    has_left, has_right = ty > 0, ty < NY - 1
    half = TW // 2
    near, far = pl.ds(0, half), pl.ds(half, half)
    moves = [
        (strips.at[pl.ds(2, 2)], got_strips.at[0], (0, 1), has_right, has_left),
        (strips.at[pl.ds(0, 2)], got_strips.at[1], (0, -1), has_left, has_right),
        (edges.at[1, :, far], got_corners.at[0], (1, 1), has_down & has_right, has_up & has_left),
        (edges.at[1, :, near], got_corners.at[1], (1, -1), has_down & has_left, has_up & has_right),
        (edges.at[0, :, far], got_corners.at[2], (-1, 1), has_up & has_right, has_down & has_left),
        (edges.at[0, :, near], got_corners.at[3], (-1, -1), has_up & has_left, has_down & has_right),
        (edges.at[1], got_edges.at[0], (1, 0), has_down, has_up),
        (edges.at[0], got_edges.at[1], (-1, 0), has_up, has_down),
    ]
    halo = []
    for n, (source, target, (down, right), sends, receives) in enumerate(moves):
        place = (lax.rem(tx + down + NX, NX), lax.rem(ty + right + NY, NY))
        copy = pltpu.make_async_remote_copy(
            source, target, halo_send.at[n], halo_recv.at[n], device_id=place, device_id_type=MESH
        )
        pl.when(sends)(copy.start)
        halo.append((copy, sends, receives))
    def lay_middle(t):
        for a in range(3):
            start = pl.multiple_of(t * PITCH1, 8) + 22 + a
            middle[t, :, 128 * a : 128 * a + 128] = b32[pl.ds(start, MID), :].astype(BF)

    def lay_ends(t):
        for a in range(3):
            for n in range(2):
                start = pl.multiple_of(t * PITCH1, 8) + 6 + a + 128 * n
                ends[t, 16 * n : 16 * n + 16, 128 * a : 128 * a + 128] = b32[pl.ds(start, 16), :].astype(BF)

    def first_conv(source, t, columns):
        height = source.shape[1]
        pixels = [source[pl.ds(t + b, columns)].reshape(columns * height, 3 * C1) for b in range(3)]
        summed = jnp.dot(jnp.concatenate(pixels, axis=1), w1[...], preferred_element_type=F32)
        value = jnp.maximum(summed * scale1[...] + shift1[...], 0.0).astype(BF).astype(F32)
        return value.reshape(columns, height, C2)

    def loop(start, stop, step, unroll):
        def body(n, carry):
            step(n)
            return carry

        lax.fori_loop(start, stop, body, 0, unroll=unroll)

    loop(2, TW + 2, lay_middle, 5)
    for copy in weight_loads:
        copy.wait()

    def middle_block(n):
        t = 2 + n * CB
        value = first_conv(middle, t, CB)
        for m in range(CB):
            for c in range(2):
                h32[c, pl.ds(16 * PITCH2 + t + m, MID, stride=PITCH2), :] = value[m, :, 128 * c : 128 * c + 128]

    loop(0, (TW - 2) // CB, middle_block, 1)

    for copy, _, receives in halo:
        pl.when(receives)(copy.wait_recv)

    for side, inside in ((0, has_up), (1, has_down)):
        for r in range(2):
            row = 6 + r + side * (TR + 2)
            line = jnp.where(inside, got_edges[side, r].astype(F32), 0.0)
            b32[pl.ds(2 * PITCH1 + row, TW, stride=PITCH1), :] = line
    for side, inside in ((0, has_left), (1, has_right)):
        for c in range(2):
            start = (c + side * (TW + 2)) * PITCH1
            strip = jnp.where(inside, got_strips[side, c].astype(F32), 0.0)
            b32[start + 8 : start + 8 + TR] = strip
    for corner in range(4):
        lower, to_left = corner >= 2, corner % 2 == 0
        inside = (has_down if lower else has_up) & (has_left if to_left else has_right)
        for r in range(2):
            values = jnp.where(inside, got_corners[corner, r].astype(F32), 0.0)
            for c in range(2):
                column = c if to_left else TW + 2 + c
                picked = half - 2 + c if to_left else c
                at = column * PITCH1 + 6 + r + (TR + 2 if lower else 0)
                b32[at : at + 1] = values[picked : picked + 1]

    loop(0, TW + 4, lay_ends, 4)
    for t in (0, 1, TW + 2, TW + 3):
        lay_middle(t)

    for t, inside in ((0, has_left), (TW, has_right)):
        value = first_conv(middle, t, 2)
        for m in range(2):
            kept = value[m]
            if t + m in (0, TW + 1):
                kept = jnp.where(inside, kept, 0.0)
            for c in range(2):
                h32[c, pl.ds(16 * PITCH2 + t + m, MID, stride=PITCH2), :] = kept[:, 128 * c : 128 * c + 128]

    rows = iota((32, C2), 0)
    keep_rows = ((rows > 0) | has_up) & ((rows < 17) | has_down)
    value = first_conv(ends, 0, TW + 2)
    for t in range(TW + 2):
        keep = keep_rows
        if t in (0, TW + 1):
            keep = keep & (has_right if t else has_left)
        kept = jnp.where(keep, value[t], 0.0)
        for c in range(2):
            lanes = slice(128 * c, 128 * c + 128)
            h32[c, pl.ds(t, 16, stride=PITCH2), :] = kept[:16, lanes]
            h32[c, pl.ds(128 * PITCH2 + t, 2, stride=PITCH2), :] = kept[16:18, lanes]

    exchange.wait_send()
    for copy, sends, _ in halo:
        pl.when(sends)(copy.wait_send)


def second_kernel(h32, w2, scale2, shift2, out_h, l2, out, out_sem):
    def move(n, y, size):
        part = pl.ds(y, size)
        return pltpu.make_async_copy(out.at[part], out_h.at[part], out_sem.at[n])

    def lay_row(h):
        for b in range(3):
            for c in range(2):
                lanes = 256 * b + 128 * c
                l2[h, :, lanes : lanes + 128] = h32[c, h * PITCH2 + b : h * PITCH2 + b + TW, :].astype(BF)

    y, laid = 0, 0
    moves = []
    for n, size in enumerate(PARTS):
        for h in range(laid, y + size + 2):
            lay_row(h)
        laid = y + size + 2
        summed = None
        for a in range(3):
            pixels = l2[y + a : y + a + size].reshape(size * TW, 3 * C2)
            part = jnp.dot(pixels, w2[3 * C2 * a : 3 * C2 * (a + 1)], preferred_element_type=F32)
            summed = part if a == 0 else summed + part
        value = jnp.maximum(summed * scale2[...] + shift2[...], 0.0).astype(BF)
        out[y : y + size] = value.reshape(size, TW, C2)
        moves.append(move(n, y, size))
        moves[-1].start()
        y += size
    for copy in moves:
        copy.wait()


def per_device(
    scenes, foot_tile, foot_offset, foot_count, row_weight, stem_weight, stem_bias,
    first_weight, first_scale, first_shift, second_weight, second_scale, second_shift,
):
    args = (
        scenes.reshape(2 * TR, 3 * 128),
        foot_tile.reshape(1, ENT),
        foot_offset.reshape(1, ENT),
        foot_count.reshape(1, ENT),
        row_weight.reshape(1, 128),
        stem_weight,
        stem_bias.reshape(1, C1),
        first_weight,
        first_scale.reshape(1, C2),
        first_shift.reshape(1, C2),
    )
    dma = pltpu.SemaphoreType.DMA
    v = pltpu.VMEM
    scratch = [v(x.shape, x.dtype) for x in args]
    scratch += [
        v((3, 264, 128), F32), v((DEV * 16, 128), F32), v((DEV, 16, 128), BF), v((DEV, 16, 128), BF),
        v((DEV * 16, 128), F32), v((384, 1024), F32), v((384, 1024), BF),
        v(((TW + 4) * PITCH1, 128), F32), v((4, TR, 128), BF), v((2, 2, TW, 128), BF),
        v((2, 2, TR, 128), BF), v((2, 2, TW, 128), BF), v((4, 2, TW // 2, 128), BF),
        v((TW + 4, MID, 384), BF), v((TW + 4, 32, 384), BF),
        dma, dma((8,)), dma((9,)), dma, dma, dma((8,)), dma((8,)),
    ]
    hidden = pl.pallas_call(
        kernel,
        out_shape=jax.ShapeDtypeStruct((2, (TR + 2) * PITCH2, 128), F32),
        in_specs=[pl.BlockSpec(memory_space=pltpu.HBM)] * len(args),
        out_specs=pl.BlockSpec(memory_space=v),
        scratch_shapes=scratch,
        compiler_params=pltpu.CompilerParams(
            collective_id=0, has_side_effects=True, vmem_limit_bytes=44 * 1024 * 1024
        ),
        cost_estimate=pl.CostEstimate(flops=2_700_000_000, bytes_accessed=2_000_000, transcendentals=0),
    )(*[pltpu.with_memory_space_constraint(x, pltpu.HBM) for x in args])
    return pl.pallas_call(
        second_kernel,
        out_shape=jax.ShapeDtypeStruct((TR, TW, C2), BF),
        in_specs=[pl.BlockSpec(memory_space=v)] * 4,
        out_specs=pl.BlockSpec(memory_space=pl.ANY),
        scratch_shapes=[v((TR + 2, TW, 3 * C2), BF), v((TR, TW, C2), BF), dma((len(PARTS),))],
        compiler_params=pltpu.CompilerParams(vmem_limit_bytes=32 * 1024 * 1024),
        cost_estimate=pl.CostEstimate(flops=4_800_000_000, bytes_accessed=3_000_000, transcendentals=0),
    )(hidden, second_weight, second_scale.reshape(1, C2), second_shift.reshape(1, C2))


def solution(mesh):
    shared = P()
    split = P(("tx", "ty"))
    in_specs = (P(("tx", "ty"), None, None), split, split, split, split) + (shared,) * 8
    return jax.shard_map(
        per_device, mesh=mesh, in_specs=in_specs, out_specs=P("tx", "ty", None), check_vma=False
    )
```

```python
import jax
import jax.numpy as jnp
from jax import lax
from jax.experimental import pallas as pl
from jax.experimental.pallas import tpu as pltpu
from jax.sharding import PartitionSpec as P

TR, TW = 128, 32
NX, NY = 8, 16
DEV = NX * NY
ENT = 64
C1, C2 = 128, 256
PITCH1 = 152
PITCH2 = 40
MID = 128
CB = 15
PARTS = (32, 32, 32, 32)
BF, F32 = jnp.bfloat16, jnp.float32
MESH = pl.DeviceIdType.MESH


def iota(shape, dim):
    return lax.broadcasted_iota(jnp.int32, shape, dim)


def far_first(tx, ty):
    y, core = tx // 2, lax.rem(tx, 2)
    z, x = ty // 4, lax.rem(ty, 4)
    ys, zs, xs = ([lax.rem(at + d, 4) for d in range(4)] for at in (y, z, x))
    cores = [core, 1 - core]
    steps = [(a, b, c, d) for a in range(4) for b in range(4) for c in range(4) for d in range(2)][1:]
    steps.sort(key=lambda s: (-sum(min(n, 4 - n) for n in s[:3]), s[3], s))
    return [(ys[a] * 2 + cores[d], zs[b] * 4 + xs[c]) for a, b, c, d in steps]


def pack_messages(scene, tile, offset, count, rweight, s32, o32, out):
    for c in range(3):
        s32[c, 0:8] = jnp.zeros((8, 128), F32)
        s32[c, 8:264] = scene[:, 128 * c : 128 * c + 128].astype(F32)
    first_row = (iota((ENT, 128), 0) % (ENT // 2)) != 0
    chunks = []
    for p in range(5):
        for c in range(3):
            rows = s32[c, pl.ds(7 + p, ENT, stride=4), :]
            if p == 0:
                rows = jnp.where(first_row, rows, 0.0)
            chunks.append(rows.astype(BF))
    pixels = jnp.concatenate(chunks, axis=1)
    onehot = (iota((DEV, ENT), 0) == tile[...]).astype(F32).astype(BF)
    picked = jnp.dot(onehot, pixels, preferred_element_type=F32)
    for r in range(15):
        o32[pl.ds(r, DEV, stride=16), :] = picked[:, 128 * r : 128 * r + 128]
    both = jnp.broadcast_to(rweight[...].astype(F32), (16, 128)).astype(BF)
    src, dst = iota((128, ENT), 0), iota((128, ENT), 1)
    w0 = jnp.dot(both, (src == 2 * dst).astype(F32).astype(BF), preferred_element_type=F32)[0:1]
    w1 = jnp.dot(both, (src == 2 * dst + 1).astype(F32).astype(BF), preferred_element_type=F32)[0:1]
    row = iota((TR, ENT), 0)
    spread = jnp.where(row == offset[...], w0, 0.0)
    spread += jnp.where(row == offset[...] + 1, jnp.where(count[...] > 1, w1 + 16.0, 0.0), 0.0)
    o32[pl.ds(15, DEV, stride=16), :] = lax.dot_general(
        onehot, spread.astype(BF), (((1,), (1,)), ((), ())), preferred_element_type=F32
    )
    out[...] = o32[...].astype(BF).reshape(DEV, 16, 128)


def build_stem(stem_w, wf, wide):
    wf[...] = jnp.zeros(wf.shape, F32)
    taps = stem_w[...].astype(F32)
    for a in range(3):
        for j in range(8):
            wf[128 * a + 12 * j : 128 * a + 12 * j + 18, 128 * j : 128 * j + 128] = taps[18 * a : 18 * a + 18]
    wide[...] = wf[...].astype(BF)


def blend(arrived, r32, wide, bias, b32, strips):
    r32[...] = arrived[...].astype(F32).reshape(DEV * 16, 128)

    def chunk(r):
        return r32[pl.ds(r, DEV, stride=16), :]

    lane = iota((DEV, 128), 1)
    windows = []
    for p in range(5):
        c0, c1, c2 = chunk(3 * p), chunk(3 * p + 1), chunk(3 * p + 2)
        w0 = jnp.where(lane < 6, 0.0, pltpu.roll(c0, 6, 1))
        w1 = jnp.where(lane < 38, pltpu.roll(c0, 38, 1), pltpu.roll(c1, 38, 1))
        w2 = jnp.where(lane < 70, pltpu.roll(c1, 70, 1), pltpu.roll(c2, 70, 1))
        w3 = pltpu.roll(c2, 102, 1)
        windows.append([w.astype(BF) for w in (w0, w1, w2, w3)])
    code = chunk(15)
    first = jnp.where(code <= 8.0, code, 0.0)
    second = jnp.where(code > 8.0, code - 16.0, 0.0)
    weights = jnp.concatenate([first, second], axis=0).astype(BF)
    contract = (((0,), (0,)), ((), ()))
    total = lax.dot_general(weights, jnp.ones((256, 128), BF), contract, preferred_element_type=F32)
    inverse = 1.0 / jnp.maximum(total, 1.0)
    wide_bias = jnp.concatenate([bias[...]] * 8, axis=1)
    for m in range(4):
        pixels = jnp.concatenate(
            [jnp.concatenate([windows[2 * i + a][m] for a in range(3)], axis=1) for i in range(2)], axis=0
        )
        summed = jnp.dot(pixels, wide[...], preferred_element_type=F32) + wide_bias
        features = jnp.maximum(summed, 0.0).astype(BF)
        numerator = lax.dot_general(weights, features, contract, preferred_element_type=F32)
        for j in range(8):
            column = 8 * m + j
            value = (numerator[:, 128 * j : 128 * j + 128] * inverse).astype(BF)
            start = (column + 2) * PITCH1 + 8
            b32[start : start + TR] = value.astype(F32)
            if column < 2:
                strips[column] = value
            if column >= TW - 2:
                strips[column - TW + 4] = value


def kernel(
    scene_h, tile_h, offset_h, count_h, rweight_h, stem_w_h, bias_h,
    w1_h, scale1_h, shift1_h, h32,
    scene, tile, offset, count, rweight, stem_w, bias, w1, scale1, shift1,
    s32, o32, send, recv, r32, wf, wide, b32, strips, edges, got_strips, got_edges, got_corners,
    middle, ends,
    in_sem, small_sem, w_sem, a2a_send, a2a_recv, halo_send, halo_recv,
):
    tx, ty = lax.axis_index("tx"), lax.axis_index("ty")
    me = tx * NY + ty

    small = [
        (tile_h, tile), (offset_h, offset), (count_h, count), (rweight_h, rweight), (stem_w_h, stem_w), (bias_h, bias),
        (scale1_h, scale1), (shift1_h, shift1),
    ]
    loads = [pltpu.make_async_copy(scene_h, scene, in_sem)]
    loads += [pltpu.make_async_copy(a, b, small_sem.at[n]) for n, (a, b) in enumerate(small)]
    for copy in loads:
        copy.start()
    weight_loads = []
    for a in range(3):
        for b in range(3):
            source, target = (3 * a + b) * C1, (3 * b + a) * C1
            weight_loads.append(
                pltpu.make_async_copy(w1_h.at[pl.ds(source, C1)], w1.at[pl.ds(target, C1)], w_sem.at[3 * a + b])
            )
    for copy in weight_loads:
        copy.start()

    barrier = pltpu.get_barrier_semaphore()
    places = far_first(tx, ty)
    for place in places:
        pl.semaphore_signal(barrier, inc=1, device_id=place, device_id_type=MESH)

    for copy in loads:
        copy.wait()
    pack_messages(scene, tile, offset, count, rweight, s32, o32, send)

    pl.semaphore_wait(barrier, DEV - 1)
    for place in places:
        pltpu.make_async_remote_copy(
            send.at[place[0] * NY + place[1]], recv.at[me], a2a_send, a2a_recv, device_id=place, device_id_type=MESH
        ).start()
    recv[me] = send[me]
    build_stem(stem_w, wf, wide)
    others = pl.ds(0, DEV - 1)
    exchange = pltpu.make_async_remote_copy(
        send.at[others], recv.at[others], a2a_send, a2a_recv, device_id=(tx, ty), device_id_type=MESH
    )
    exchange.wait_recv()

    blend(recv, r32, wide, bias, b32, strips)

    for side in range(2):
        for r in range(2):
            row = 8 + r + side * (TR - 2)
            edges[side, r] = b32[pl.ds(2 * PITCH1 + row, TW, stride=PITCH1), :].astype(BF)
    has_up, has_down = tx > 0, tx < NX - 1
    has_left, has_right = ty > 0, ty < NY - 1
    half = TW // 2
    near, far = pl.ds(0, half), pl.ds(half, half)
    moves = [
        (strips.at[pl.ds(2, 2)], got_strips.at[0], (0, 1), has_right, has_left),
        (strips.at[pl.ds(0, 2)], got_strips.at[1], (0, -1), has_left, has_right),
        (edges.at[1, :, far], got_corners.at[0], (1, 1), has_down & has_right, has_up & has_left),
        (edges.at[1, :, near], got_corners.at[1], (1, -1), has_down & has_left, has_up & has_right),
        (edges.at[0, :, far], got_corners.at[2], (-1, 1), has_up & has_right, has_down & has_left),
        (edges.at[0, :, near], got_corners.at[3], (-1, -1), has_up & has_left, has_down & has_right),
        (edges.at[1], got_edges.at[0], (1, 0), has_down, has_up),
        (edges.at[0], got_edges.at[1], (-1, 0), has_up, has_down),
    ]
    halo = []
    for n, (source, target, (down, right), sends, receives) in enumerate(moves):
        place = (lax.rem(tx + down + NX, NX), lax.rem(ty + right + NY, NY))
        copy = pltpu.make_async_remote_copy(
            source, target, halo_send.at[n], halo_recv.at[n], device_id=place, device_id_type=MESH
        )
        pl.when(sends)(copy.start)
        halo.append((copy, sends, receives))
    def lay_middle(t):
        for a in range(3):
            start = pl.multiple_of(t * PITCH1, 8) + 7 + a
            middle[t, :, 128 * a : 128 * a + 128] = b32[pl.ds(start, MID), :].astype(BF)

    def finish_first(pixels):
        summed = jnp.dot(pixels, w1[...], preferred_element_type=F32)
        return jnp.maximum(summed * scale1[...] + shift1[...], 0.0).astype(BF).astype(F32)

    def first_conv(source, t, columns):
        height = source.shape[1]
        pixels = [source[pl.ds(t + b, columns)].reshape(columns * height, 3 * C1) for b in range(3)]
        value = finish_first(jnp.concatenate(pixels, axis=1))
        return value.reshape(columns, height, C2)

    def loop(start, stop, step, unroll):
        def body(n, carry):
            step(n)
            return carry

        lax.fori_loop(start, stop, body, 0, unroll=unroll)

    loop(2, TW + 2, lay_middle, 5)
    for copy in weight_loads:
        copy.wait()

    def middle_block(n):
        t = 2 + n * CB
        value = first_conv(middle, t, CB)
        for m in range(CB):
            for c in range(2):
                h32[c, pl.ds(PITCH2 + t + m, MID, stride=PITCH2), :] = value[m, :, 128 * c : 128 * c + 128]

    loop(0, (TW - 2) // CB, middle_block, 1)

    for copy, _, receives in halo:
        pl.when(receives)(copy.wait_recv)

    for side, inside in ((0, has_up), (1, has_down)):
        for r in range(2):
            row = 6 + r + side * (TR + 2)
            line = jnp.where(inside, got_edges[side, r].astype(F32), 0.0)
            b32[pl.ds(2 * PITCH1 + row, TW, stride=PITCH1), :] = line
    for side, inside in ((0, has_left), (1, has_right)):
        for c in range(2):
            start = (c + side * (TW + 2)) * PITCH1
            strip = jnp.where(inside, got_strips[side, c].astype(F32), 0.0)
            b32[start + 8 : start + 8 + TR] = strip
    for corner in range(4):
        lower, to_left = corner >= 2, corner % 2 == 0
        inside = (has_down if lower else has_up) & (has_left if to_left else has_right)
        for r in range(2):
            values = jnp.where(inside, got_corners[corner, r].astype(F32), 0.0)
            for c in range(2):
                column = c if to_left else TW + 2 + c
                picked = half - 2 + c if to_left else c
                at = column * PITCH1 + 6 + r + (TR + 2 if lower else 0)
                b32[at : at + 1] = values[picked : picked + 1]

    for t in (0, 1, TW + 2, TW + 3):
        lay_middle(t)

    for n, h in enumerate((0, 1, TR, TR + 1)):
        for b in range(3):
            for a in range(3):
                line = b32[pl.ds(b * PITCH1 + 6 + h + a, TW + 2, stride=PITCH1), :]
                lanes = 128 * (3 * b + a)
                ends[n, : TW + 2, lanes : lanes + 128] = line.astype(BF)
    pixels = [
        jnp.concatenate([middle[pl.ds(t + b, 2)].reshape(2 * MID, 3 * C1) for b in range(3)], axis=1) for t in (0, TW)
    ]
    both = finish_first(jnp.concatenate(pixels + [ends[...].reshape(4 * 48, 9 * C1)], axis=0))
    for n, (t, inside) in enumerate(((0, has_left), (1, True), (TW, True), (TW + 1, has_right))):
        kept = both[MID * n : MID * n + MID]
        if t in (0, TW + 1):
            kept = jnp.where(inside, kept, 0.0)
        for c in range(2):
            h32[c, pl.ds(PITCH2 + t, MID, stride=PITCH2), :] = kept[:, 128 * c : 128 * c + 128]
    value = both[4 * MID :].reshape(4, 48, C2)
    columns = iota((48, C2), 0)
    keep_columns = ((columns > 0) | has_left) & ((columns < TW + 1) | has_right)
    for n, (h, inside) in enumerate(((0, has_up), (1, True), (TR, True), (TR + 1, has_down))):
        kept = jnp.where(keep_columns & inside, value[n], 0.0)
        for c in range(2):
            h32[c, h * PITCH2 : h * PITCH2 + TW + 2] = kept[: TW + 2, 128 * c : 128 * c + 128]

    exchange.wait_send()
    for copy, sends, _ in halo:
        pl.when(sends)(copy.wait_send)


def second_kernel(h32, w2, scale2, shift2, out_h, l2, out, out_sem):
    def move(n, y, size):
        part = pl.ds(y, size)
        return pltpu.make_async_copy(out.at[part], out_h.at[part], out_sem.at[n])

    def lay_row(h):
        for b in range(3):
            for c in range(2):
                lanes = 256 * b + 128 * c
                l2[h, :, lanes : lanes + 128] = h32[c, h * PITCH2 + b : h * PITCH2 + b + TW, :].astype(BF)

    y, laid = 0, 0
    moves = []
    for n, size in enumerate(PARTS):
        for h in range(laid, y + size + 2):
            lay_row(h)
        laid = y + size + 2
        summed = None
        for a in range(3):
            pixels = l2[y + a : y + a + size].reshape(size * TW, 3 * C2)
            part = jnp.dot(pixels, w2[3 * C2 * a : 3 * C2 * (a + 1)], preferred_element_type=F32)
            summed = part if a == 0 else summed + part
        value = jnp.maximum(summed * scale2[...] + shift2[...], 0.0).astype(BF)
        out[y : y + size] = value.reshape(size, TW, C2)
        moves.append(move(n, y, size))
        moves[-1].start()
        y += size
    for copy in moves:
        copy.wait()


def per_device(
    scenes, foot_tile, foot_offset, foot_count, row_weight, stem_weight, stem_bias,
    first_weight, first_scale, first_shift, second_weight, second_scale, second_shift,
):
    args = (
        scenes.reshape(2 * TR, 3 * 128),
        foot_tile.reshape(1, ENT),
        foot_offset.reshape(1, ENT),
        foot_count.reshape(1, ENT),
        row_weight.reshape(1, 128),
        stem_weight,
        stem_bias.reshape(1, C1),
        first_weight,
        first_scale.reshape(1, C2),
        first_shift.reshape(1, C2),
    )
    dma = pltpu.SemaphoreType.DMA
    v = pltpu.VMEM
    scratch = [v(x.shape, x.dtype) for x in args]
    scratch += [
        v((3, 264, 128), F32), v((DEV * 16, 128), F32), v((DEV, 16, 128), BF), v((DEV, 16, 128), BF),
        v((DEV * 16, 128), F32), v((384, 1024), F32), v((384, 1024), BF),
        v(((TW + 4) * PITCH1, 128), F32), v((4, TR, 128), BF), v((2, 2, TW, 128), BF),
        v((2, 2, TR, 128), BF), v((2, 2, TW, 128), BF), v((4, 2, TW // 2, 128), BF),
        v((TW + 4, MID, 384), BF), v((4, 48, 9 * C1), BF),
        dma, dma((8,)), dma((9,)), dma, dma, dma((8,)), dma((8,)),
    ]
    hidden = pl.pallas_call(
        kernel,
        out_shape=jax.ShapeDtypeStruct((2, (TR + 2) * PITCH2, 128), F32),
        in_specs=[pl.BlockSpec(memory_space=pltpu.HBM)] * len(args),
        out_specs=pl.BlockSpec(memory_space=v),
        scratch_shapes=scratch,
        compiler_params=pltpu.CompilerParams(
            collective_id=0, has_side_effects=True, vmem_limit_bytes=44 * 1024 * 1024
        ),
        cost_estimate=pl.CostEstimate(flops=2_700_000_000, bytes_accessed=2_000_000, transcendentals=0),
    )(*[pltpu.with_memory_space_constraint(x, pltpu.HBM) for x in args])
    return pl.pallas_call(
        second_kernel,
        out_shape=jax.ShapeDtypeStruct((TR, TW, C2), BF),
        in_specs=[pl.BlockSpec(memory_space=v)] * 4,
        out_specs=pl.BlockSpec(memory_space=pl.ANY),
        scratch_shapes=[v((TR + 2, TW, 3 * C2), BF), v((TR, TW, C2), BF), dma((len(PARTS),))],
        compiler_params=pltpu.CompilerParams(vmem_limit_bytes=32 * 1024 * 1024),
        cost_estimate=pl.CostEstimate(flops=4_800_000_000, bytes_accessed=3_000_000, transcendentals=0),
    )(hidden, second_weight, second_scale.reshape(1, C2), second_shift.reshape(1, C2))


def solution(mesh):
    shared = P()
    split = P(("tx", "ty"))
    in_specs = (P(("tx", "ty"), None, None), split, split, split, split) + (shared,) * 8
    return jax.shard_map(
        per_device, mesh=mesh, in_specs=in_specs, out_specs=P("tx", "ty", None), check_vma=False
    )
```

```python
import jax
import jax.numpy as jnp
from jax import lax
from jax.experimental import pallas as pl
from jax.experimental.pallas import tpu as pltpu
from jax.sharding import PartitionSpec as P

TR, TW = 128, 32
NX, NY = 8, 16
DEV = NX * NY
ENT = 64
C1, C2 = 128, 256
PITCH1 = 152
PITCH2 = 40
MID = 128
CB = 5
PARTS = (32, 32, 32, 32)
BF, F32 = jnp.bfloat16, jnp.float32
MESH = pl.DeviceIdType.MESH


def iota(shape, dim):
    return lax.broadcasted_iota(jnp.int32, shape, dim)


def far_first(tx, ty):
    y, core = tx // 2, lax.rem(tx, 2)
    z, x = ty // 4, lax.rem(ty, 4)
    ys, zs, xs = ([lax.rem(at + d, 4) for d in range(4)] for at in (y, z, x))
    cores = [core, 1 - core]
    steps = [(a, b, c, d) for a in range(4) for b in range(4) for c in range(4) for d in range(2)][1:]
    steps.sort(key=lambda s: (-sum(min(n, 4 - n) for n in s[:3]), s[3], s))
    return [(ys[a] * 2 + cores[d], zs[b] * 4 + xs[c]) for a, b, c, d in steps]


def pack_messages(scene, tile, offset, count, rweight, s32, o32, out):
    for c in range(3):
        s32[c, 0:8] = jnp.zeros((8, 128), F32)
        s32[c, 8:264] = scene[:, 128 * c : 128 * c + 128].astype(F32)
    first_row = (iota((ENT, 128), 0) % (ENT // 2)) != 0
    chunks = []
    for p in range(5):
        for c in range(3):
            rows = s32[c, pl.ds(7 + p, ENT, stride=4), :]
            if p == 0:
                rows = jnp.where(first_row, rows, 0.0)
            chunks.append(rows.astype(BF))
    pixels = jnp.concatenate(chunks, axis=1)
    onehot = (iota((DEV, ENT), 0) == tile[...]).astype(F32).astype(BF)
    picked = jnp.dot(onehot, pixels, preferred_element_type=F32)
    for r in range(15):
        o32[pl.ds(r, DEV, stride=16), :] = picked[:, 128 * r : 128 * r + 128]
    both = jnp.broadcast_to(rweight[...].astype(F32), (16, 128)).astype(BF)
    src, dst = iota((128, ENT), 0), iota((128, ENT), 1)
    w0 = jnp.dot(both, (src == 2 * dst).astype(F32).astype(BF), preferred_element_type=F32)[0:1]
    w1 = jnp.dot(both, (src == 2 * dst + 1).astype(F32).astype(BF), preferred_element_type=F32)[0:1]
    row = iota((TR, ENT), 0)
    spread = jnp.where(row == offset[...], w0, 0.0)
    spread += jnp.where(row == offset[...] + 1, jnp.where(count[...] > 1, w1 + 16.0, 0.0), 0.0)
    o32[pl.ds(15, DEV, stride=16), :] = lax.dot_general(
        onehot, spread.astype(BF), (((1,), (1,)), ((), ())), preferred_element_type=F32
    )
    out[...] = o32[...].astype(BF).reshape(DEV, 16, 128)


def build_stem(stem_w, wf, wide):
    wf[...] = jnp.zeros(wf.shape, F32)
    taps = stem_w[...].astype(F32)
    for a in range(3):
        for j in range(8):
            wf[128 * a + 12 * j : 128 * a + 12 * j + 18, 128 * j : 128 * j + 128] = taps[18 * a : 18 * a + 18]
    wide[...] = wf[...].astype(BF)


def blend(arrived, r32, wide, bias, b32, strips):
    r32[...] = arrived[...].astype(F32).reshape(DEV * 16, 128)

    def chunk(r):
        return r32[pl.ds(r, DEV, stride=16), :]

    lane = iota((DEV, 128), 1)
    windows = []
    for p in range(5):
        c0, c1, c2 = chunk(3 * p), chunk(3 * p + 1), chunk(3 * p + 2)
        w0 = jnp.where(lane < 6, 0.0, pltpu.roll(c0, 6, 1))
        w1 = jnp.where(lane < 38, pltpu.roll(c0, 38, 1), pltpu.roll(c1, 38, 1))
        w2 = jnp.where(lane < 70, pltpu.roll(c1, 70, 1), pltpu.roll(c2, 70, 1))
        w3 = pltpu.roll(c2, 102, 1)
        windows.append([w.astype(BF) for w in (w0, w1, w2, w3)])
    code = chunk(15)
    first = jnp.where(code <= 8.0, code, 0.0)
    second = jnp.where(code > 8.0, code - 16.0, 0.0)
    weights = jnp.concatenate([first, second], axis=0).astype(BF)
    contract = (((0,), (0,)), ((), ()))
    total = lax.dot_general(weights, jnp.ones((256, 128), BF), contract, preferred_element_type=F32)
    inverse = 1.0 / jnp.maximum(total, 1.0)
    wide_bias = jnp.concatenate([bias[...]] * 8, axis=1)
    for m in range(4):
        pixels = jnp.concatenate(
            [jnp.concatenate([windows[2 * i + a][m] for a in range(3)], axis=1) for i in range(2)], axis=0
        )
        summed = jnp.dot(pixels, wide[...], preferred_element_type=F32) + wide_bias
        features = jnp.maximum(summed, 0.0).astype(BF)
        numerator = lax.dot_general(weights, features, contract, preferred_element_type=F32)
        for j in range(8):
            column = 8 * m + j
            value = (numerator[:, 128 * j : 128 * j + 128] * inverse).astype(BF)
            start = (column + 2) * PITCH1 + 8
            b32[start : start + TR] = value.astype(F32)
            if column < 2:
                strips[column] = value
            if column >= TW - 2:
                strips[column - TW + 4] = value


def kernel(
    scene_h, tile_h, offset_h, count_h, rweight_h, stem_w_h, bias_h,
    w1_h, scale1_h, shift1_h, h32,
    scene, tile, offset, count, rweight, stem_w, bias, w1, scale1, shift1,
    s32, o32, send, recv, r32, wf, wide, b32, strips, edges, got_strips, got_edges, got_corners,
    middle, ends,
    in_sem, small_sem, w_sem, a2a_send, a2a_recv, halo_send, halo_recv,
):
    tx, ty = lax.axis_index("tx"), lax.axis_index("ty")
    me = tx * NY + ty

    small = [
        (tile_h, tile), (offset_h, offset), (count_h, count), (rweight_h, rweight), (stem_w_h, stem_w), (bias_h, bias),
        (scale1_h, scale1), (shift1_h, shift1),
    ]
    loads = [pltpu.make_async_copy(scene_h, scene, in_sem)]
    loads += [pltpu.make_async_copy(a, b, small_sem.at[n]) for n, (a, b) in enumerate(small)]
    for copy in loads:
        copy.start()
    weight_loads = []
    for a in range(3):
        for b in range(3):
            source, target = (3 * a + b) * C1, (3 * b + a) * C1
            weight_loads.append(
                pltpu.make_async_copy(w1_h.at[pl.ds(source, C1)], w1.at[pl.ds(target, C1)], w_sem.at[3 * a + b])
            )
    for copy in weight_loads:
        copy.start()

    barrier = pltpu.get_barrier_semaphore()
    places = far_first(tx, ty)
    for place in places:
        pl.semaphore_signal(barrier, inc=1, device_id=place, device_id_type=MESH)

    for copy in loads:
        copy.wait()
    pack_messages(scene, tile, offset, count, rweight, s32, o32, send)

    pl.semaphore_wait(barrier, DEV - 1)
    for place in places:
        pltpu.make_async_remote_copy(
            send.at[place[0] * NY + place[1]], recv.at[me], a2a_send, a2a_recv, device_id=place, device_id_type=MESH
        ).start()
    recv[me] = send[me]
    build_stem(stem_w, wf, wide)
    others = pl.ds(0, DEV - 1)
    exchange = pltpu.make_async_remote_copy(
        send.at[others], recv.at[others], a2a_send, a2a_recv, device_id=(tx, ty), device_id_type=MESH
    )
    exchange.wait_recv()

    blend(recv, r32, wide, bias, b32, strips)

    for side in range(2):
        for r in range(2):
            row = 8 + r + side * (TR - 2)
            edges[side, r] = b32[pl.ds(2 * PITCH1 + row, TW, stride=PITCH1), :].astype(BF)
    has_up, has_down = tx > 0, tx < NX - 1
    has_left, has_right = ty > 0, ty < NY - 1
    half = TW // 2
    near, far = pl.ds(0, half), pl.ds(half, half)
    moves = [
        (strips.at[pl.ds(2, 2)], got_strips.at[0], (0, 1), has_right, has_left),
        (strips.at[pl.ds(0, 2)], got_strips.at[1], (0, -1), has_left, has_right),
        (edges.at[1, :, far], got_corners.at[0], (1, 1), has_down & has_right, has_up & has_left),
        (edges.at[1, :, near], got_corners.at[1], (1, -1), has_down & has_left, has_up & has_right),
        (edges.at[0, :, far], got_corners.at[2], (-1, 1), has_up & has_right, has_down & has_left),
        (edges.at[0, :, near], got_corners.at[3], (-1, -1), has_up & has_left, has_down & has_right),
        (edges.at[1], got_edges.at[0], (1, 0), has_down, has_up),
        (edges.at[0], got_edges.at[1], (-1, 0), has_up, has_down),
    ]
    halo = []
    for n, (source, target, (down, right), sends, receives) in enumerate(moves):
        place = (lax.rem(tx + down + NX, NX), lax.rem(ty + right + NY, NY))
        copy = pltpu.make_async_remote_copy(
            source, target, halo_send.at[n], halo_recv.at[n], device_id=place, device_id_type=MESH
        )
        pl.when(sends)(copy.start)
        halo.append((copy, sends, receives))
    def lay_middle(t):
        for a in range(3):
            start = t * PITCH1 + 7 + a
            middle[t, :, 128 * a : 128 * a + 128] = b32[start : start + MID].astype(BF)

    def finish_first(pixels):
        summed = jnp.dot(pixels, w1[...], preferred_element_type=F32)
        return jnp.maximum(summed * scale1[...] + shift1[...], 0.0).astype(BF).astype(F32)

    def first_conv(source, t, columns):
        height = source.shape[1]
        pixels = [source[t + b : t + b + columns].reshape(columns * height, 3 * C1) for b in range(3)]
        value = finish_first(jnp.concatenate(pixels, axis=1))
        return value.reshape(columns, height, C2)

    for copy in weight_loads:
        copy.wait()

    laid = 2
    for t in range(2, TW, CB):
        for column in range(laid, t + CB + 2):
            lay_middle(column)
        laid = t + CB + 2
        value = first_conv(middle, t, CB)
        for m in range(CB):
            for c in range(2):
                h32[c, pl.ds(PITCH2 + t + m, MID, stride=PITCH2), :] = value[m, :, 128 * c : 128 * c + 128]

    for copy, _, receives in halo:
        pl.when(receives)(copy.wait_recv)

    for side, inside in ((0, has_up), (1, has_down)):
        for r in range(2):
            row = 6 + r + side * (TR + 2)
            line = jnp.where(inside, got_edges[side, r].astype(F32), 0.0)
            b32[pl.ds(2 * PITCH1 + row, TW, stride=PITCH1), :] = line
    for side, inside in ((0, has_left), (1, has_right)):
        for c in range(2):
            start = (c + side * (TW + 2)) * PITCH1
            strip = jnp.where(inside, got_strips[side, c].astype(F32), 0.0)
            b32[start + 8 : start + 8 + TR] = strip
    for corner in range(4):
        lower, to_left = corner >= 2, corner % 2 == 0
        inside = (has_down if lower else has_up) & (has_left if to_left else has_right)
        for r in range(2):
            values = jnp.where(inside, got_corners[corner, r].astype(F32), 0.0)
            for c in range(2):
                column = c if to_left else TW + 2 + c
                picked = half - 2 + c if to_left else c
                at = column * PITCH1 + 6 + r + (TR + 2 if lower else 0)
                b32[at : at + 1] = values[picked : picked + 1]

    for t in (0, 1, TW + 2, TW + 3):
        lay_middle(t)

    for n, h in enumerate((0, 1, TR, TR + 1)):
        for b in range(3):
            for a in range(3):
                line = b32[pl.ds(b * PITCH1 + 6 + h + a, TW + 2, stride=PITCH1), :]
                lanes = 128 * (3 * b + a)
                ends[n, : TW + 2, lanes : lanes + 128] = line.astype(BF)
    pixels = [
        jnp.concatenate([middle[pl.ds(t + b, 2)].reshape(2 * MID, 3 * C1) for b in range(3)], axis=1) for t in (0, TW)
    ]
    both = finish_first(jnp.concatenate(pixels + [ends[...].reshape(4 * 48, 9 * C1)], axis=0))
    for n, (t, inside) in enumerate(((0, has_left), (1, True), (TW, True), (TW + 1, has_right))):
        kept = both[MID * n : MID * n + MID]
        if t in (0, TW + 1):
            kept = jnp.where(inside, kept, 0.0)
        for c in range(2):
            h32[c, pl.ds(PITCH2 + t, MID, stride=PITCH2), :] = kept[:, 128 * c : 128 * c + 128]
    value = both[4 * MID :].reshape(4, 48, C2)
    columns = iota((48, C2), 0)
    keep_columns = ((columns > 0) | has_left) & ((columns < TW + 1) | has_right)
    for n, (h, inside) in enumerate(((0, has_up), (1, True), (TR, True), (TR + 1, has_down))):
        kept = jnp.where(keep_columns & inside, value[n], 0.0)
        for c in range(2):
            h32[c, h * PITCH2 : h * PITCH2 + TW + 2] = kept[: TW + 2, 128 * c : 128 * c + 128]

    exchange.wait_send()
    for copy, sends, _ in halo:
        pl.when(sends)(copy.wait_send)


def second_kernel(h32, w2, scale2, shift2, out_h, l2, out, out_sem):
    def move(n, y, size):
        part = pl.ds(y, size)
        return pltpu.make_async_copy(out.at[part], out_h.at[part], out_sem.at[n])

    def lay_row(h):
        for b in range(3):
            for c in range(2):
                lanes = 256 * b + 128 * c
                l2[h, :, lanes : lanes + 128] = h32[c, h * PITCH2 + b : h * PITCH2 + b + TW, :].astype(BF)

    y, laid = 0, 0
    moves = []
    for n, size in enumerate(PARTS):
        for h in range(laid, y + size + 2):
            lay_row(h)
        laid = y + size + 2
        summed = None
        for a in range(3):
            pixels = l2[y + a : y + a + size].reshape(size * TW, 3 * C2)
            part = jnp.dot(pixels, w2[3 * C2 * a : 3 * C2 * (a + 1)], preferred_element_type=F32)
            summed = part if a == 0 else summed + part
        value = jnp.maximum(summed * scale2[...] + shift2[...], 0.0).astype(BF)
        out[y : y + size] = value.reshape(size, TW, C2)
        moves.append(move(n, y, size))
        moves[-1].start()
        y += size
    for copy in moves:
        copy.wait()


def per_device(
    scenes, foot_tile, foot_offset, foot_count, row_weight, stem_weight, stem_bias,
    first_weight, first_scale, first_shift, second_weight, second_scale, second_shift,
):
    args = (
        scenes.reshape(2 * TR, 3 * 128),
        foot_tile.reshape(1, ENT),
        foot_offset.reshape(1, ENT),
        foot_count.reshape(1, ENT),
        row_weight.reshape(1, 128),
        stem_weight,
        stem_bias.reshape(1, C1),
        first_weight,
        first_scale.reshape(1, C2),
        first_shift.reshape(1, C2),
    )
    dma = pltpu.SemaphoreType.DMA
    v = pltpu.VMEM
    scratch = [v(x.shape, x.dtype) for x in args]
    scratch += [
        v((3, 264, 128), F32), v((DEV * 16, 128), F32), v((DEV, 16, 128), BF), v((DEV, 16, 128), BF),
        v((DEV * 16, 128), F32), v((384, 1024), F32), v((384, 1024), BF),
        v(((TW + 4) * PITCH1, 128), F32), v((4, TR, 128), BF), v((2, 2, TW, 128), BF),
        v((2, 2, TR, 128), BF), v((2, 2, TW, 128), BF), v((4, 2, TW // 2, 128), BF),
        v((TW + 4, MID, 384), BF), v((4, 48, 9 * C1), BF),
        dma, dma((8,)), dma((9,)), dma, dma, dma((8,)), dma((8,)),
    ]
    hidden = pl.pallas_call(
        kernel,
        out_shape=jax.ShapeDtypeStruct((2, (TR + 2) * PITCH2, 128), F32),
        in_specs=[pl.BlockSpec(memory_space=pltpu.HBM)] * len(args),
        out_specs=pl.BlockSpec(memory_space=v),
        scratch_shapes=scratch,
        compiler_params=pltpu.CompilerParams(
            collective_id=0, has_side_effects=True, vmem_limit_bytes=44 * 1024 * 1024
        ),
        cost_estimate=pl.CostEstimate(flops=2_700_000_000, bytes_accessed=2_000_000, transcendentals=0),
    )(*[pltpu.with_memory_space_constraint(x, pltpu.HBM) for x in args])
    return pl.pallas_call(
        second_kernel,
        out_shape=jax.ShapeDtypeStruct((TR, TW, C2), BF),
        in_specs=[pl.BlockSpec(memory_space=v)] * 4,
        out_specs=pl.BlockSpec(memory_space=pl.ANY),
        scratch_shapes=[v((TR + 2, TW, 3 * C2), BF), v((TR, TW, C2), BF), dma((len(PARTS),))],
        compiler_params=pltpu.CompilerParams(vmem_limit_bytes=32 * 1024 * 1024),
        cost_estimate=pl.CostEstimate(flops=4_800_000_000, bytes_accessed=3_000_000, transcendentals=0),
    )(hidden, second_weight, second_scale.reshape(1, C2), second_shift.reshape(1, C2))


def solution(mesh):
    shared = P()
    split = P(("tx", "ty"))
    in_specs = (P(("tx", "ty"), None, None), split, split, split, split) + (shared,) * 8
    return jax.shard_map(
        per_device, mesh=mesh, in_specs=in_specs, out_specs=P("tx", "ty", None), check_vma=False
    )
```
